512 devices in a mesh: gx: 8 (over y, core), gy: 64 (over x, z).
Axes of the slice: x: 4, y: 4, z: 16, core: 2. Of those that a mesh axis runs over, the one named last changes fastest.
Arguments:
- coords: bfloat16 [3, 2097152], P(None, ('gx', 'gy')), may hold values from -6 to 6
- vectors: float32 [16, 2097152], P(None, ('gx', 'gy')), may hold values from -6 to 6
- basis: bfloat16 [4096, 512, 128], P(('gx', 'gy')), may hold values from -0.25 to 0.25
- leaf_up: bfloat16 [4096, 128, 128], P(('gx', 'gy')), may hold values from -0.1875 to 0.1875
- mid_up: bfloat16 [512, 128, 128], P(('gx', 'gy')), may hold values from -0.1875 to 0.1875
- top_up: bfloat16 [64, 128, 128], P('gx'), may hold values from -0.1875 to 0.1875
- couple_one: bfloat16 [512, 6, 128, 128], P(('gx', 'gy')), may hold values from -0.21875 to 0.21875
- couple_two: bfloat16 [64, 6, 128, 128], P('gx'), may hold values from -0.21875 to 0.21875
- couple_three: bfloat16 [8, 6, 128, 128], P('gx'), may hold values from -0.21875 to 0.21875
- far_one: int32 [512, 6], P(('gx', 'gy')), may hold values from 0 to 63
- far_two: int32 [64, 6], P('gx'), may hold values from 0 to 7
- far_three: int32 [8, 6], P('gx'), may hold values from 0 to 7
- near_list: int32 [4096, 16], P(('gx', 'gy')), may hold values from 0 to 23
- near_count: int32 [4096], P(('gx', 'gy')), may hold values from 1 to 16, as said below
Outputs:
- product: float32 [16, 2097152], P(None, ('gx', 'gy'))
The draws below stay inside these ranges and needn't reach their ends.
Inputs may be any that keep to these rules, and one draw needn't show every extreme that they name: `near_count`: each leaf box has 1 to 16 live near slots; some box has 16 in every draw; loads differ from device to device.
All inputs are finite; a program needn't handle non-finite values.
Results may differ from the reference program's by a relative error of at most 0.007.
Values may be sent and summed in bfloat16 or wider, within the bound.
A program may use at most 64 MiB of HBM per device.

```python
import jax
import jax.numpy as jnp
from jax import lax

P_SIZE = 512
R = 128
Q = 16
BOX_DEV = 8
NEAR = 16
FAR = 6
NBOX = 4096
NPTS = 2097152
N1 = 512
GROUPS = 8
N2 = 64
N_GX = 8
N_GY = 64


def draw_near_count(key, part):
    key = jax.random.fold_in(key, 7)
    first, second = jax.random.split(key)
    level = jax.random.randint(first, (NBOX // BOX_DEV, 1), 1, NEAR + 1)
    counts = jax.random.randint(second, (NBOX // BOX_DEV, BOX_DEV), 0, NEAR) % level + 1
    counts = counts.at[0, 0].set(NEAR)
    return counts.reshape(NBOX).astype(jnp.int32)


def plant(values, key, low, high):
    dims = values.shape
    place = [jax.random.randint(jax.random.fold_in(key, axis), (), 0, dims[axis]) for axis in range(len(dims))]
    values = values.at[tuple(place)].set(low)
    longest = dims.index(max(dims))
    place[longest] = (place[longest] + 1) % dims[longest]
    return values.at[tuple(place)].set(high)


def steps_of(rng, dims, cuts, least, top_value):
    factor_of, own = 1.0, jax.random.fold_in(rng, 6)
    for axis_at, shards_of in cuts:
        steps = jnp.exp(jax.random.uniform(jax.random.fold_in(own, axis_at), (shards_of,), jnp.float32, least / len(cuts), top_value / len(cuts)))
        factor_of = factor_of * jnp.repeat(steps, dims[axis_at] // shards_of).reshape([-1 if axis == axis_at else 1 for axis in range(len(dims))])
    return factor_of


def normal_values(stream_key, shape, spread, limit, pieces=(), held_as=jnp.bfloat16):
    drawn = spread * jax.random.normal(stream_key, shape, jnp.float32)
    if pieces:
        drawn = drawn * steps_of(stream_key, shape, pieces, -0.22, 0.18)
    return jnp.clip(drawn, -limit, limit).astype(held_as)


def setup_inputs(seed: int = 0) -> dict:
    seeds = jax.random.split(jax.random.key(seed), 15)
    coords = normal_values(seeds[0], (3, NPTS), 1.0, 6.0, ((1, 512),))
    vectors = normal_values(seeds[1], (Q, NPTS), 1.0, 6.0, ((1, 512),), jnp.float32)
    basis = normal_values(seeds[2], (NBOX, P_SIZE, R), P_SIZE ** -0.5, 0.25, ((0, 512),))
    leaf_up = normal_values(seeds[3], (NBOX, R, R), (8 * R) ** -0.5, 0.1875, ((0, 512),))
    mid_up = normal_values(seeds[4], (N1, R, R), (8 * R) ** -0.5, 0.1875, ((0, 512),))
    top_up = normal_values(seeds[5], (N2, R, R), (R * GROUPS) ** -0.5, 0.1875, ((0, 8),))
    couple_one = normal_values(seeds[6], (N1, FAR, R, R), (R * FAR) ** -0.5, 0.21875, ((0, 512),))
    couple_two = normal_values(seeds[7], (N2, FAR, R, R), (R * FAR) ** -0.5, 0.21875, ((0, 8),))
    couple_three = normal_values(seeds[8], (N_GX, FAR, R, R), (R * FAR) ** -0.5, 0.21875, ((0, 8),))
    far_one = plant(jax.random.randint(seeds[9], (N1, FAR), 0, N_GY), jax.random.fold_in(seeds[9], 1), 0, N_GY - 1).astype(jnp.int32)
    far_two = plant(jax.random.randint(seeds[10], (N2, FAR), 0, GROUPS), jax.random.fold_in(seeds[10], 1), 0, GROUPS - 1).astype(jnp.int32)
    far_three = plant(jax.random.randint(seeds[11], (N_GX, FAR), 0, N_GX), jax.random.fold_in(seeds[11], 1), 0, N_GX - 1).astype(jnp.int32)
    near_list = plant(jax.random.randint(seeds[12], (NBOX, NEAR), 0, 3 * BOX_DEV), jax.random.fold_in(seeds[12], 1), 0, (3 * BOX_DEV) - 1).astype(jnp.int32)
    near_count = draw_near_count(jax.random.fold_in(seeds[14], 71), 0)
    return dict(coords=coords, vectors=vectors, basis=basis, leaf_up=leaf_up, mid_up=mid_up, top_up=top_up, couple_one=couple_one, couple_two=couple_two, couple_three=couple_three, far_one=far_one, far_two=far_two, far_three=far_three, near_list=near_list, near_count=near_count)


def rounded(value):
    return lax.optimization_barrier(value.astype(jnp.bfloat16)).astype(jnp.float32)

def kernel_tile(targets, sources):
    dist_sq = jnp.zeros((targets.shape[1], targets.shape[2], sources.shape[2]), jnp.float32)
    for comp in range(3):
        delta = targets[comp][:, :, None] - sources[comp][:, None, :]
        dist_sq = dist_sq + delta * delta
    return jnp.exp(-jnp.sqrt(dist_sq)).astype(jnp.bfloat16)

def reference(coords, vectors, basis, leaf_up, mid_up, top_up, couple_one, couple_two, couple_three, far_one, far_two, far_three, near_list, near_count):
    devices = N_GX * N_GY
    groups = N_GY // 8
    pack = jnp.concatenate([coords.astype(jnp.float32), vectors], axis=0).reshape(3 + Q, NBOX, P_SIZE)
    boxes_of = vectors.reshape(Q, NBOX, P_SIZE)

    def lower(dev):
        start = (dev * BOX_DEV).astype(jnp.int32)
        own_vec = lax.dynamic_slice_in_dim(boxes_of, start, BOX_DEV, 1)
        own_basis = lax.dynamic_slice_in_dim(basis, start, BOX_DEV, 0).astype(jnp.float32)
        own_up = lax.dynamic_slice_in_dim(leaf_up, start, BOX_DEV, 0).astype(jnp.float32)
        leaf = jnp.einsum('qbp,bpr->bqr', rounded(own_vec), own_basis)
        return jnp.einsum('bqr,brs->qs', rounded(leaf), own_up)
    level_one = lax.map(lower, jnp.arange(devices, dtype=jnp.int32))
    mid_f = mid_up.astype(jnp.float32)
    up_two = jnp.einsum('iqr,irs->iqs', rounded(level_one), mid_f)
    level_two = up_two.reshape(N_GX, groups, 8, Q, R).sum(axis=2)
    tops = top_up.astype(jnp.float32).reshape(N_GX, groups, R, R)
    level_three = jnp.einsum('gjqr,gjrs->gqs', rounded(level_two), tops)
    local_three = jnp.einsum('gfqr,gfrs->gqs', rounded(level_three[far_three]), couple_three.astype(jnp.float32))
    rows = jnp.arange(N_GX, dtype=jnp.int32)[:, None, None]
    src_two = level_two[rows, far_two.reshape(N_GX, groups, FAR)]
    local_two = jnp.einsum('gjfqr,gjfrs->gjqs', rounded(src_two), couple_two.astype(jnp.float32).reshape(N_GX, groups, FAR, R, R))
    local_two = local_two + jnp.einsum('gqs,gjrs->gjqr', rounded(local_three), tops)
    src_one = level_one.reshape(N_GX, N_GY, Q, R)[rows, far_one.reshape(N_GX, N_GY, FAR)].reshape(devices, FAR, Q, R)
    local_one = jnp.einsum('ifqr,ifrs->iqs', rounded(src_one), couple_one.astype(jnp.float32))
    parents = local_two.reshape(N_GX * groups, Q, R)[jnp.arange(devices, dtype=jnp.int32) // 8]
    local_one = local_one + jnp.einsum('iqs,irs->iqr', rounded(parents), mid_f)

    def upper(dev):
        start = (dev * BOX_DEV).astype(jnp.int32)
        column = dev % N_GY
        own_basis = lax.dynamic_slice_in_dim(basis, start, BOX_DEV, 0).astype(jnp.float32)
        own_up = lax.dynamic_slice_in_dim(leaf_up, start, BOX_DEV, 0).astype(jnp.float32)
        mine = lax.dynamic_index_in_dim(local_one, dev, 0, keepdims=False)
        local_leaf = jnp.einsum('qs,brs->bqr', rounded(mine), own_up)
        far_part = jnp.einsum('bqr,bpr->qbp', rounded(local_leaf), own_basis)
        targets = lax.dynamic_slice_in_dim(pack, start, BOX_DEV, 1)[:3]
        lists = lax.dynamic_slice_in_dim(near_list, start, BOX_DEV, 0)
        counts = lax.dynamic_slice_in_dim(near_count, start, BOX_DEV, 0)

        def slot(step, total):
            index = lax.dynamic_index_in_dim(lists, step, 1, keepdims=False)
            side = index // BOX_DEV - 1
            inside = (column + side >= 0) & (column + side < N_GY) & (step < counts)
            source = jnp.clip(start - BOX_DEV + index, 0, NBOX - 1).astype(jnp.int32)
            sources = jnp.take(pack, source, axis=1)
            tile = kernel_tile(targets, sources[:3]).astype(jnp.float32)
            values = rounded(jnp.where(inside[None, :, None], sources[3:], 0.0))
            return total + jnp.einsum('bts,qbs->qbt', tile, values)
        near_part = lax.fori_loop(0, NEAR, slot, jnp.zeros((Q, BOX_DEV, P_SIZE), jnp.float32))
        return (near_part * P_SIZE ** (-0.5) + far_part).reshape(Q, BOX_DEV * P_SIZE)
    result = lax.map(upper, jnp.arange(devices, dtype=jnp.int32))
    return jnp.transpose(result, (1, 0, 2)).reshape(Q, NPTS)
```

```python
import functools
import math

import jax
import jax.numpy as jnp
from jax import lax
from jax.experimental import pallas as pl
from jax.experimental.pallas import tpu as pltpu
from jax.sharding import PartitionSpec as P

MESH = pl.DeviceIdType.MESH
F32 = jnp.float32
BF = jnp.bfloat16
BOXES = 8
POINTS = 512
PROBES = 16
RANK = 128
NEAR = 16
FAR = 6
WIDTH = BOXES * POINTS
GROUP = 8
ANY = pl.BlockSpec(memory_space=pl.ANY)
VMEM = pl.BlockSpec(memory_space=pltpu.VMEM)
SMEM = pl.BlockSpec(memory_space=pltpu.SMEM)


def dot(a, b):
    return jnp.dot(a, b, preferred_element_type=F32)


def dot_t(a, b):
    return lax.dot_general(a, b, (((1,), (1,)), ((), ())), preferred_element_type=F32)


def gather(ref, index_of):
    return jnp.concatenate([ref[index_of(f)] for f in range(FAR)], axis=1)


def far_kernel(
    gy_count,
    coords,
    vectors,
    basis_hbm,
    leaf_hbm,
    mid_hbm,
    top_hbm,
    one_hbm,
    two_hbm,
    three_hbm,
    far_one,
    far_two,
    far_three,
    side_vec,
    side_pos,
    far_out,
    basis,
    leaf_up,
    mid_up,
    top_up,
    couple_one,
    couple_two,
    couple_three,
    vec,
    pos_f32,
    pos,
    family,
    level_two,
    level_three,
    row_one,
    load_sem,
    side_send,
    side_recv,
    family_send,
    family_recv,
    two_send,
    two_recv,
    row_send,
    row_recv,
    three_send,
    three_recv,
):
    gx = lax.axis_index("gx")
    gy = lax.axis_index("gy")
    group = gy // GROUP
    member = gy % GROUP
    loads = [
        pltpu.make_async_copy(source, target, load_sem.at[n])
        for n, (source, target) in enumerate(
            (
                (basis_hbm, basis),
                (leaf_hbm, leaf_up),
                (mid_hbm, mid_up),
                (top_hbm, top_up),
                (two_hbm.at[group], couple_two),
                (three_hbm, couple_three),
                (one_hbm, couple_one),
            )
        )
    ]
    for load in loads:
        load.start()

    right = (gy + 1) % gy_count
    left = (gy + gy_count - 1) % gy_count

    def in_family(step):
        return group * GROUP + (member + step) % GROUP

    def in_groups(step):
        return ((group + step) % GROUP) * GROUP + member

    barrier = pltpu.get_barrier_semaphore()
    for peer in (left, right):
        pl.semaphore_signal(barrier, inc=1, device_id=(gx, peer), device_id_type=MESH)

    def greet(step, carry):
        for peer in ((gx, in_family(step)), (gx, in_groups(step)), ((gx + step) % 8, gy)):
            pl.semaphore_signal(barrier, inc=1, device_id=peer, device_id_type=MESH)
        return carry

    lax.fori_loop(1, 8, greet, 0)

    vec[...] = vectors[...].astype(BF)
    for comp in range(3):
        for box in range(BOXES):
            row = comp * BOXES + box
            pos_f32[row : row + 1, :] = coords[comp : comp + 1, box * POINTS : (box + 1) * POINTS].astype(F32)
    pos_f32[24:32, :] = jnp.zeros((8, POINTS), F32)
    pos[...] = pos_f32[...].astype(BF)

    loads[0].wait()
    loads[1].wait()
    leaf = jnp.concatenate(
        [dot(vec[:, b * POINTS : (b + 1) * POINTS], basis[b]).astype(BF) for b in range(BOXES)], axis=1
    )
    ups = leaf_up[...].reshape(BOXES * RANK, RANK)
    one = dot(leaf, ups).astype(BF)
    loads[2].wait()
    toward = dot(one, mid_up[0])
    family[member] = jnp.concatenate([one, toward.astype(BF)], axis=0)

    pl.semaphore_wait(barrier, 23)

    def family_copy(step, slot):
        return pltpu.make_async_remote_copy(
            src_ref=family.at[member],
            dst_ref=family.at[member],
            send_sem=family_send.at[step],
            recv_sem=family_recv.at[slot],
            device_id=(gx, in_family(step)),
            device_id_type=MESH,
        )

    def two_copy(step, slot):
        return pltpu.make_async_remote_copy(
            src_ref=level_two.at[group],
            dst_ref=level_two.at[group],
            send_sem=two_send.at[step],
            recv_sem=two_recv.at[slot],
            device_id=(gx, in_groups(step)),
            device_id_type=MESH,
        )

    def row_copy(step, slot):
        part = row_one.at[pl.ds(group * GROUP, GROUP)]
        return pltpu.make_async_remote_copy(
            src_ref=part,
            dst_ref=part,
            send_sem=row_send.at[step],
            recv_sem=row_recv.at[slot],
            device_id=(gx, in_groups(step)),
            device_id_type=MESH,
        )

    def three_copy(step, slot):
        return pltpu.make_async_remote_copy(
            src_ref=level_three.at[gx],
            dst_ref=level_three.at[gx],
            send_sem=three_send.at[step],
            recv_sem=three_recv.at[slot],
            device_id=((gx + step) % 8, gy),
            device_id_type=MESH,
        )

    def start_all(copy, mine):
        def start(step, carry):
            copy(step, mine).start()
            return carry

        lax.fori_loop(1, 8, start, 0)

    def arrive_all(copy, mine):
        def arrive(step, carry):
            copy(step, (mine + step) % 8).wait_recv()
            return carry

        lax.fori_loop(1, 8, arrive, 0)

    def sent_all(copy, mine):
        def sent(step, carry):
            copy(step, mine).wait_send()
            return carry

        lax.fori_loop(1, 8, sent, 0)

    start_all(family_copy, member)

    sides = []
    for n, (source, target) in enumerate(((vec, side_vec), (pos, side_pos))):
        for side, peer in ((0, right), (1, left)):
            sides.append(
                pltpu.make_async_remote_copy(
                    src_ref=source,
                    dst_ref=target.at[side],
                    send_sem=side_send.at[2 * n + side],
                    recv_sem=side_recv.at[2 * n + side],
                    device_id=(gx, peer),
                    device_id_type=MESH,
                )
            )
    for copy in sides:
        copy.start()

    arrive_all(family_copy, member)
    two = jnp.zeros((PROBES, RANK), F32)
    for n in range(GROUP):
        two = two + family[n, PROBES:, :].astype(F32)
        row_one[group * GROUP + n] = family[n, :PROBES, :]
    level_two[group] = two.astype(BF)
    start_all(two_copy, group)
    start_all(row_copy, group)

    loads[3].wait()
    arrive_all(two_copy, group)
    twos = jnp.concatenate([level_two[n] for n in range(8)], axis=1)
    level_three[gx] = dot(twos, top_up[...].reshape(8 * RANK, RANK)).astype(BF)
    start_all(three_copy, gx)

    loads[4].wait()
    local_two = dot(gather(level_two, lambda f: far_two[group, f]), couple_two[...].reshape(FAR * RANK, RANK))
    loads[5].wait()
    loads[6].wait()
    arrive_all(row_copy, group)
    local_one = dot(gather(row_one, lambda f: far_one[0, f]), couple_one[0].reshape(FAR * RANK, RANK))

    arrive_all(three_copy, gx)
    local_three = dot(gather(level_three, lambda f: far_three[0, f]), couple_three[0].reshape(FAR * RANK, RANK))
    local_two = local_two + dot_t(local_three.astype(BF), top_up[group])
    local_one = local_one + dot_t(local_two.astype(BF), mid_up[0])
    local_leaf = dot_t(local_one.astype(BF), ups).astype(BF)
    for b in range(BOXES):
        far_out[:, b * POINTS : (b + 1) * POINTS] = dot_t(local_leaf[:, b * RANK : (b + 1) * RANK], basis[b])

    for copy in sides:
        copy.wait()
    sent_all(family_copy, member)
    sent_all(two_copy, group)
    sent_all(row_copy, group)
    sent_all(three_copy, gx)


def far_field(gy_count, coords, vectors, basis, leaf_up, mid_up, top_up, one, two, three, far_one, far_two, far_three):
    dma = pltpu.SemaphoreType.DMA
    return pl.pallas_call(
        functools.partial(far_kernel, gy_count),
        out_shape=(
            jax.ShapeDtypeStruct((2, PROBES, WIDTH), BF),
            jax.ShapeDtypeStruct((2, 32, POINTS), BF),
            jax.ShapeDtypeStruct((PROBES, WIDTH), F32),
        ),
        in_specs=[VMEM, VMEM] + [ANY] * 7 + [SMEM] * 3,
        out_specs=(ANY, ANY, VMEM),
        scratch_shapes=[
            pltpu.VMEM((BOXES, POINTS, RANK), BF),
            pltpu.VMEM((BOXES, RANK, RANK), BF),
            pltpu.VMEM((1, RANK, RANK), BF),
            pltpu.VMEM((8, RANK, RANK), BF),
            pltpu.VMEM((1, FAR, RANK, RANK), BF),
            pltpu.VMEM((FAR, RANK, RANK), BF),
            pltpu.VMEM((1, FAR, RANK, RANK), BF),
            pltpu.VMEM((PROBES, WIDTH), BF),
            pltpu.VMEM((32, POINTS), F32),
            pltpu.VMEM((32, POINTS), BF),
            pltpu.VMEM((8, 2 * PROBES, RANK), BF),
            pltpu.VMEM((8, PROBES, RANK), BF),
            pltpu.VMEM((8, PROBES, RANK), BF),
            pltpu.VMEM((64, PROBES, RANK), BF),
            dma((7,)),
            dma((4,)),
            dma((4,)),
            dma((8,)),
            dma((8,)),
            dma((8,)),
            dma((8,)),
            dma((8,)),
            dma((8,)),
            dma((8,)),
            dma((8,)),
        ],
        compiler_params=pltpu.CompilerParams(
            collective_id=0, has_side_effects=True, vmem_limit_bytes=40 << 20
        ),
    )(coords, vectors, basis, leaf_up, mid_up, top_up, one, two, three, far_one, far_two, far_three)


def lanes(box):
    return pl.ds(pl.multiple_of(box * POINTS, POINTS), POINTS)


def near_kernel(
    gy_count,
    near_list,
    near_count,
    coords,
    vectors,
    side_vec,
    side_pos,
    far_part,
    out,
    pos,
    raw,
    source,
    target,
    vec,
    dist,
    times,
    task_box,
    task_from,
):
    gy = lax.axis_index("gy")

    def clear(n, carry):
        for k in range(8):
            times[n * 8 + k] = 0
        return carry

    lax.fori_loop(0, 24, clear, 0)
    tasks = jnp.int32(0)
    for box in range(BOXES):

        def add(slot, tasks, box=box):
            place = near_list[box, slot]
            column = gy + place // BOXES - 1
            known = times[box * 24 + place]
            times[box * 24 + place] = known + 1
            task_box[tasks] = box
            task_from[tasks] = place
            fresh = (known == 0) & (column >= 0) & (column < gy_count)
            return tasks + jnp.where(fresh, 1, 0)

        tasks = lax.fori_loop(0, near_count[box], add, tasks)
    for k in range(4):
        task_box[tasks + k] = 0
        task_from[tasks + k] = BOXES

    for comp in range(3):
        for box in range(BOXES):
            row = comp * BOXES + box
            pos[1, row : row + 1, :] = coords[comp : comp + 1, box * POINTS : (box + 1) * POINTS].astype(F32)
    pos[0] = side_pos[0].astype(F32)
    pos[2] = side_pos[1].astype(F32)
    raw[...] = jnp.zeros_like(raw)
    ones = jnp.ones((3, WIDTH), F32)
    for third in range(3):
        parts = [pos[third, comp * BOXES : (comp + 1) * BOXES, :] for comp in range(3)]
        norm = parts[0] * parts[0] + parts[1] * parts[1] + parts[2] * parts[2]
        high = norm.astype(BF).astype(F32)
        rest = norm - high
        middle = rest.astype(BF).astype(F32)
        low = rest - middle
        rows = [-2.0 * part for part in parts] + [high, middle, low]
        for box in range(BOXES):
            for n, value in enumerate(rows):
                raw[n : n + 1, box * POINTS : (box + 1) * POINTS] = value[box : box + 1, :]
        raw[6:9, :] = ones
        source[:, third * WIDTH : (third + 1) * WIDTH] = raw[...].astype(BF)
        if third == 1:
            for box in range(BOXES):
                for n, value in enumerate(parts):
                    raw[n : n + 1, box * POINTS : (box + 1) * POINTS] = value[box : box + 1, :]
                for n, value in enumerate((high, middle, low)):
                    raw[n + 6 : n + 7, box * POINTS : (box + 1) * POINTS] = value[box : box + 1, :]
            raw[3:6, :] = ones
            target[...] = raw[...].astype(BF)
    vec[:, :WIDTH] = side_vec[0]
    vec[:, WIDTH : 2 * WIDTH] = vectors[...].astype(BF)
    vec[:, 2 * WIDTH :] = side_vec[1]

    out[...] = far_part[...]

    def squares(task):
        return lax.dot_general(
            source[:, lanes(task_from[task])],
            target[:, lanes(task_box[task])],
            (((0,), (0,)), ((), ())),
            preferred_element_type=F32,
        )

    dist[0] = squares(0)

    def step(turn, carry):
        for k in range(4):
            task = turn * 4 + k
            square = jnp.maximum(dist[k % 2], 1e-30)
            dist[1 - k % 2] = squares(task + 1)
            tile = jnp.exp2((square * -math.log2(math.e)) * lax.rsqrt(square)).astype(BF)
            box = task_box[task]
            place = task_from[task]
            count = jnp.where(task < tasks, times[box * 24 + place], 0)
            weight = count.astype(F32) * POINTS**-0.5
            out[:, lanes(box)] += weight * dot(vec[:, lanes(place)], tile)
        return carry

    lax.fori_loop(0, (tasks + 3) // 4, step, 0)


def near_field(gy_count, near_list, near_count, coords, vectors, side_vec, side_pos, far_part):
    return pl.pallas_call(
        functools.partial(near_kernel, gy_count),
        out_shape=jax.ShapeDtypeStruct((PROBES, WIDTH), F32),
        in_specs=[SMEM, SMEM] + [VMEM] * 5,
        out_specs=VMEM,
        scratch_shapes=[
            pltpu.VMEM((3, 32, POINTS), F32),
            pltpu.VMEM((16, WIDTH), F32),
            pltpu.VMEM((16, 3 * WIDTH), BF),
            pltpu.VMEM((16, WIDTH), BF),
            pltpu.VMEM((PROBES, 3 * WIDTH), BF),
            pltpu.VMEM((2, POINTS, POINTS), F32),
            pltpu.SMEM((192,), jnp.int32),
            pltpu.SMEM((136,), jnp.int32),
            pltpu.SMEM((136,), jnp.int32),
        ],
        compiler_params=pltpu.CompilerParams(vmem_limit_bytes=40 << 20),
    )(near_list, near_count, coords, vectors, side_vec, side_pos, far_part)


def local(gy_count, *args):
    coords, vectors, basis, leaf_up, mid_up, top_up = args[:6]
    couple_one, couple_two, couple_three, far_one, far_two, far_three, near_list, near_count = args[6:]
    side_vec, side_pos, far_part = far_field(
        gy_count,
        coords,
        vectors,
        basis,
        leaf_up,
        mid_up,
        top_up,
        couple_one,
        couple_two,
        couple_three,
        far_one,
        far_two,
        far_three,
    )
    return near_field(gy_count, near_list, near_count, coords, vectors, side_vec, side_pos, far_part)


def solution(mesh):
    both = ("gx", "gy")
    return jax.shard_map(
        functools.partial(local, mesh.shape["gy"]),
        mesh=mesh,
        in_specs=(
            P(None, both),
            P(None, both),
            P(both, None, None),
            P(both, None, None),
            P(both, None, None),
            P("gx", None, None),
            P(both, None, None, None),
            P("gx", None, None, None),
            P("gx", None, None, None),
            P(both, None),
            P("gx", None),
            P("gx", None),
            P(both, None),
            P(both),
        ),
        out_specs=P(None, both),
        check_vma=False,
    )
```

```python
import functools
import math

import jax
import jax.numpy as jnp
from jax import lax
from jax.experimental import pallas as pl
from jax.experimental.pallas import tpu as pltpu
from jax.sharding import PartitionSpec as P

MESH = pl.DeviceIdType.MESH
F32 = jnp.float32
BF = jnp.bfloat16
I32 = jnp.int32
BOXES = 8
POINTS = 512
PROBES = 16
RANK = 128
NEAR = 16
FAR = 6
WIDTH = BOXES * POINTS
GX = 8
LINE = 16
LINES = 4
GROUP = 8
TURN = 4
OWN_TURNS = 7
MID_TURNS = 2
LAST_TURNS = 2
OWN_DONE = OWN_TURNS * TURN
SIDE_DONE = (MID_TURNS + LAST_TURNS) * TURN
SCALE = POINTS**-0.5
VMEM_LIMIT = 63 << 20
HBM = pl.BlockSpec(memory_space=pltpu.HBM)
VMEM = pl.BlockSpec(memory_space=pltpu.VMEM)
SMEM = pl.BlockSpec(memory_space=pltpu.SMEM)


def dot(a, b):
    return jnp.dot(a, b, preferred_element_type=F32)


def dot_t(a, b):
    return lax.dot_general(a, b, (((1,), (1,)), ((), ())), preferred_element_type=F32)


def span(box):
    return slice(box * POINTS, (box + 1) * POINTS)


def gather(ref, index_of):
    return jnp.concatenate([ref[index_of(f)] for f in range(FAR)], axis=1)


def squares(source, target):
    return lax.dot_general(source, target, (((0,), (0,)), ((), ())), preferred_element_type=F32)


def tile_of(square):
    square = jnp.maximum(square, 1e-30)
    return jnp.exp2((square * -math.log2(math.e)) * lax.rsqrt(square)).astype(BF)


def norm_parts(parts):
    norm = parts[0] * parts[0] + parts[1] * parts[1] + parts[2] * parts[2]
    high = norm.astype(BF).astype(F32)
    rest = norm - high
    middle = rest.astype(BF).astype(F32)
    return [high, middle, rest - middle]


def set_rows(raw, first, values):
    for n, value in enumerate(values):
        for box in range(BOXES):
            raw[box, first + n : first + n + 1, :] = value[box : box + 1, :]


def compact(times, box, place):
    count = times.shape[0]
    across = lax.broadcasted_iota(I32, (count, 128), 1)
    down = lax.broadcasted_iota(I32, (count, 128), 0)
    live = jnp.broadcast_to(jnp.where(times > 0, 1, 0), (count, 128))
    along = jnp.sum(jnp.where(across == down, live, 0), axis=0, keepdims=True)
    rank = jnp.sum(jnp.where(across < down, along, 0), axis=1, keepdims=True)
    hit = (rank == across) & (live > 0)
    rows = [jnp.sum(jnp.where(hit, value, 0), axis=0, keepdims=True) for value in (box, place, times)]
    return rows, jnp.sum(live, axis=0, keepdims=True)


def pair_lists(near_list, near_count, gy, gy_count, out):
    place = lax.broadcasted_iota(I32, (3 * BOXES, NEAR), 0)
    slot = lax.broadcasted_iota(I32, (3 * BOXES, NEAR), 1)
    column = gy + place // BOXES - 1
    inside = (column >= 0) & (column < gy_count)
    own, side = [], []
    for box in range(BOXES):
        named = (near_list[box : box + 1, :] == place) & (slot < near_count[box]) & inside
        times = jnp.sum(jnp.where(named, 1, 0), axis=1, keepdims=True)
        own.append(times[BOXES : 2 * BOXES])
        side += [times[:BOXES], times[2 * BOXES :]]
    own, side = jnp.concatenate(own, axis=0), jnp.concatenate(side, axis=0)
    n = lax.broadcasted_iota(I32, own.shape, 0)
    own_rows, own_count = compact(own, n // BOXES, n % BOXES)
    n = lax.broadcasted_iota(I32, side.shape, 0)
    side_rows, side_count = compact(side, n // (2 * BOXES), n % (2 * BOXES))
    for n, row in enumerate(own_rows + side_rows + [own_count, side_count]):
        out[n : n + 1, :] = row


def far_kernel(
    gy_count,
    coords_hbm,
    vectors_hbm,
    list_hbm,
    count_hbm,
    basis_hbm,
    leaf_hbm,
    mid_hbm,
    top_hbm,
    one_hbm,
    two_hbm,
    three_hbm,
    far_one_hbm,
    far_two_hbm,
    far_three_hbm,
    total,
    pairs,
    own_vec,
    side_vec,
    own_source,
    side_source,
    target,
    coords,
    vectors,
    near_list,
    near_count,
    basis,
    leaf_up,
    mid_up,
    top_up,
    couple_one,
    couple_two,
    couple_three,
    far_one,
    far_two,
    far_three,
    pos_f32,
    pos,
    side_pos,
    raw,
    dist,
    tasks,
    toward,
    level_two,
    level_three,
    row_one,
    load_sem,
    task_sem,
    side_send,
    side_recv,
    toward_send,
    toward_recv,
    line_send,
    line_recv,
    two_send,
    two_recv,
    row_send,
    row_recv,
    three_send,
    three_recv,
):
    gx = lax.axis_index("gx")
    gy = lax.axis_index("gy")
    x = gy // LINE
    z = gy % LINE
    group = gy // GROUP
    loads = [
        pltpu.make_async_copy(source, goal, load_sem.at[n])
        for n, (source, goal) in enumerate(
            (
                (vectors_hbm, vectors),
                (coords_hbm, coords),
                (list_hbm, near_list),
                (count_hbm, near_count),
                (basis_hbm, basis),
                (leaf_hbm, leaf_up),
                (mid_hbm, mid_up),
                (top_hbm, top_up),
                (two_hbm.at[group], couple_two),
                (three_hbm, couple_three),
                (one_hbm, couple_one),
                (far_one_hbm, far_one),
                (far_two_hbm, far_two),
                (far_three_hbm, far_three),
            )
        )
    ]
    for load in loads:
        load.start()

    right = (gy + 1) % gy_count
    left = (gy + gy_count - 1) % gy_count

    def in_line(step):
        return x * LINE + (z + step) % LINE

    def in_plane(step):
        return ((x + step) % LINES) * LINE + z

    barrier = pltpu.get_barrier_semaphore()

    def greet(peer):
        pl.semaphore_signal(barrier, inc=1, device_id=peer, device_id_type=MESH)

    def greet_line(n, carry):
        greet((gx, in_line(n)))
        return carry

    def greet_three(n, carry):
        greet(((gx + n) % GX, gy))
        return carry

    lax.fori_loop(1, LINE, greet_line, 0)
    for n in range(1, LINES):
        greet((gx, in_plane(n)))
    lax.fori_loop(1, GX, greet_three, 0)
    greet((gx, left))
    greet((gx, right))

    loads[0].wait()
    for box in range(BOXES):
        own_vec[box] = vectors[:, span(box)].astype(BF)
    loads[4].wait()
    loads[5].wait()
    leaf = jnp.concatenate([dot(own_vec[b], basis[b]).astype(BF) for b in range(BOXES)], axis=1)
    ups = leaf_up[...].reshape(BOXES * RANK, RANK)
    one = dot(leaf, ups).astype(BF)
    row_one[gy] = one
    loads[6].wait()
    toward[z] = dot(one, mid_up[0]).astype(BF)

    loads[1].wait()
    for comp in range(3):
        for box in range(BOXES):
            row = comp * BOXES + box
            pos_f32[row : row + 1, :] = coords[comp : comp + 1, span(box)].astype(F32)
    pos_f32[24:32, :] = jnp.zeros((8, POINTS), F32)
    pos[...] = pos_f32[...].astype(BF)
    loads[2].wait()
    loads[3].wait()
    pair_lists(near_list, near_count, gy, gy_count, pairs)
    task_copy = pltpu.make_async_copy(pairs, tasks, task_sem.at[0])
    task_copy.start()

    raw[...] = jnp.zeros_like(raw)
    ones = [jnp.ones((BOXES, POINTS), F32)] * 3
    parts = [pos_f32[n * BOXES : (n + 1) * BOXES, :] for n in range(3)]
    norms = norm_parts(parts)
    set_rows(raw, 0, parts + ones + norms)
    target[...] = raw[...].astype(BF)
    set_rows(raw, 0, [-2.0 * part for part in parts] + norms + ones)
    own_source[...] = raw[...].astype(BF)
    total[...] = jnp.zeros_like(total)
    task_copy.wait()

    def begin(first_row, source_ref, task):
        dist[0] = squares(source_ref[tasks[first_row + 1, task]], target[tasks[first_row, task]])

    def fill(first_row, source_ref, vec_ref, first, last):
        def turn(n, carry):
            for k in range(TURN):
                task = n * TURN + k
                square = dist[k % 2]
                dist[1 - k % 2] = squares(
                    source_ref[tasks[first_row + 1, task + 1]], target[tasks[first_row, task + 1]]
                )
                part = dot(vec_ref[tasks[first_row + 1, task]], tile_of(square))
                box = tasks[first_row, task]
                weight = tasks[first_row + 2, task].astype(F32) * SCALE
                for b in range(BOXES):
                    total[:, span(b)] += jnp.where(box == b, weight, 0.0) * part
            return carry

        lax.fori_loop(first, last, turn, 0)

    ahead = (1 - z // 8) * (OWN_TURNS - z // 2) + z // 14
    begin(0, own_source, 0)
    fill(0, own_source, own_vec, 0, ahead)

    pl.semaphore_wait(barrier, LINE - 1 + LINES - 1 + GX - 1 + 2)

    def send(ref, sends, recvs, step, slot, peer):
        return pltpu.make_async_remote_copy(
            src_ref=ref,
            dst_ref=ref,
            send_sem=sends.at[step],
            recv_sem=recvs.at[slot],
            device_id=peer,
            device_id_type=MESH,
        )

    def toward_copy(step, slot):
        return send(toward.at[z], toward_send, toward_recv, step, slot, (gx, in_line(step)))

    def line_copy(step, slot):
        return send(row_one.at[gy], line_send, line_recv, step, slot, (gx, in_line(step)))

    def two_copy(step, slot):
        return send(level_two.at[x], two_send, two_recv, step, slot, (gx, in_plane(step)))

    def row_copy(step, slot):
        part = row_one.at[pl.ds(x * LINE, LINE)]
        return send(part, row_send, row_recv, step, slot, (gx, in_plane(step)))

    def three_copy(step, slot):
        return send(level_three.at[gx], three_send, three_recv, step, slot, ((gx + step) % GX, gy))

    def each(count, do):
        def body(n, carry):
            do(n)
            return carry

        lax.fori_loop(1, count, body, 0)

    def start_all(copy, mine, count):
        each(count, lambda n: copy(n, mine).start())

    def start_far_first(copy, mine):
        for n in (8, 7, 9, 6, 10, 5, 11, 4, 12, 3, 13, 2, 14, 1, 15):
            copy(n, mine).start()

    def arrive_all(copy, mine, count):
        each(count, lambda n: copy(n, (mine + n) % count).wait_recv())

    def sent_all(copy, mine, count):
        each(count, lambda n: copy(n, mine).wait_send())

    start_far_first(toward_copy, z)
    sides = []
    for n, (source, goal, rows) in enumerate(((own_vec, side_vec, 8), (pos, side_pos, 32))):
        for side, peer in ((0, right), (1, left)):
            sides.append(
                pltpu.make_async_remote_copy(
                    src_ref=source,
                    dst_ref=goal.at[pl.ds(side * rows, rows)],
                    send_sem=side_send.at[2 * n + side],
                    recv_sem=side_recv.at[2 * n + side],
                    device_id=(gx, peer),
                    device_id_type=MESH,
                )
            )
    for copy in sides:
        copy.start()
    start_far_first(line_copy, z)

    fill(0, own_source, own_vec, ahead, OWN_TURNS)

    arrive_all(toward_copy, z, LINE)
    for half in range(2):
        two = jnp.zeros((PROBES, RANK), F32)
        for n in range(GROUP):
            two = two + toward[half * GROUP + n].astype(F32)
        level_two[x, half] = two.astype(BF)
    start_all(two_copy, x, LINES)
    arrive_all(line_copy, z, LINE)
    start_all(row_copy, x, LINES)

    for copy in sides:
        copy.wait_recv()
    for side in range(2):
        first = side * 32
        near = side_pos[first : first + 24, :].astype(F32)
        parts = [near[n * BOXES : (n + 1) * BOXES, :] for n in range(3)]
        set_rows(raw, 0, [-2.0 * part for part in parts] + norm_parts(parts))
        side_source[side * BOXES : (side + 1) * BOXES] = raw[...].astype(BF)
    begin(3, side_source, 0)
    fill(3, side_source, side_vec, 0, MID_TURNS)

    loads[7].wait()
    arrive_all(two_copy, x, LINES)
    twos = jnp.concatenate([level_two[n // 2, n % 2] for n in range(8)], axis=1)
    level_three[gx] = dot(twos, top_up[...].reshape(8 * RANK, RANK)).astype(BF)
    start_all(three_copy, gx, GX)

    for load in loads[8:]:
        load.wait()
    source_two = gather(level_two, lambda f: (far_two[group, f] // 2, far_two[group, f] % 2))
    local_two = dot(source_two, couple_two[...].reshape(FAR * RANK, RANK))
    arrive_all(row_copy, x, LINES)
    local_one = dot(gather(row_one, lambda f: far_one[0, f]), couple_one[0].reshape(FAR * RANK, RANK))
    fill(3, side_source, side_vec, MID_TURNS, MID_TURNS + LAST_TURNS)

    arrive_all(three_copy, gx, GX)
    local_three = dot(gather(level_three, lambda f: far_three[0, f]), couple_three[0].reshape(FAR * RANK, RANK))
    local_two = local_two + dot_t(local_three.astype(BF), top_up[group])
    local_one = local_one + dot_t(local_two.astype(BF), mid_up[0])
    local_leaf = dot_t(local_one.astype(BF), ups).astype(BF)
    for b in range(BOXES):
        total[:, span(b)] += dot_t(local_leaf[:, b * RANK : (b + 1) * RANK], basis[b])

    for copy in sides:
        copy.wait_send()
    sent_all(toward_copy, z, LINE)
    sent_all(line_copy, z, LINE)
    sent_all(two_copy, x, LINES)
    sent_all(row_copy, x, LINES)
    sent_all(three_copy, gx, GX)


def far_field(gy_count, *arrays):
    dma = pltpu.SemaphoreType.DMA
    boxes = (BOXES, PROBES, POINTS)
    sides = (2 * BOXES, PROBES, POINTS)
    return pl.pallas_call(
        functools.partial(far_kernel, gy_count),
        out_shape=(
            jax.ShapeDtypeStruct((PROBES, WIDTH), F32),
            jax.ShapeDtypeStruct((8, 128), I32),
            jax.ShapeDtypeStruct(boxes, BF),
            jax.ShapeDtypeStruct(sides, BF),
            jax.ShapeDtypeStruct(boxes, BF),
            jax.ShapeDtypeStruct(sides, BF),
            jax.ShapeDtypeStruct(boxes, BF),
        ),
        in_specs=[HBM] * 14,
        out_specs=(VMEM,) * 7,
        scratch_shapes=[
            pltpu.VMEM((3, WIDTH), BF),
            pltpu.VMEM((PROBES, WIDTH), F32),
            pltpu.VMEM((BOXES, NEAR), I32),
            pltpu.SMEM((BOXES,), I32),
            pltpu.VMEM((BOXES, POINTS, RANK), BF),
            pltpu.VMEM((BOXES, RANK, RANK), BF),
            pltpu.VMEM((1, RANK, RANK), BF),
            pltpu.VMEM((8, RANK, RANK), BF),
            pltpu.VMEM((1, FAR, RANK, RANK), BF),
            pltpu.VMEM((FAR, RANK, RANK), BF),
            pltpu.VMEM((1, FAR, RANK, RANK), BF),
            pltpu.SMEM((1, FAR), I32),
            pltpu.SMEM((8, FAR), I32),
            pltpu.SMEM((1, FAR), I32),
            pltpu.VMEM((32, POINTS), F32),
            pltpu.VMEM((32, POINTS), BF),
            pltpu.VMEM((64, POINTS), BF),
            pltpu.VMEM(boxes, F32),
            pltpu.VMEM((2, POINTS, POINTS), F32),
            pltpu.SMEM((8, 128), I32),
            pltpu.VMEM((LINE, PROBES, RANK), BF),
            pltpu.VMEM((LINES, 2, PROBES, RANK), BF),
            pltpu.VMEM((GX, PROBES, RANK), BF),
            pltpu.VMEM((LINE * LINES, PROBES, RANK), BF),
            dma((14,)),
            dma((1,)),
            dma((4,)),
            dma((4,)),
            dma((LINE,)),
            dma((LINE,)),
            dma((LINE,)),
            dma((LINE,)),
            dma((LINES,)),
            dma((LINES,)),
            dma((LINES,)),
            dma((LINES,)),
            dma((GX,)),
            dma((GX,)),
        ],
        compiler_params=pltpu.CompilerParams(
            collective_id=0, has_side_effects=True, vmem_limit_bytes=VMEM_LIMIT
        ),
    )(*arrays)


def near_kernel(pairs, total_hbm, own_vec, side_vec, own_source, side_source, target_hbm, out, vec, source, target, dist, sem):
    loads = [
        pltpu.make_async_copy(a, b, sem.at[n])
        for n, (a, b) in enumerate(
            (
                (own_source, source.at[pl.ds(0, BOXES)]),
                (side_source, source.at[pl.ds(BOXES, 2 * BOXES)]),
                (target_hbm, target),
                (own_vec, vec.at[pl.ds(0, BOXES)]),
                (side_vec, vec.at[pl.ds(BOXES, 2 * BOXES)]),
                (total_hbm, out),
            )
        )
    ]
    for load in loads:
        load.start()
    own = jnp.maximum(pairs[6, 0] - OWN_DONE, 0)
    tasks = own + jnp.maximum(pairs[7, 0] - SIDE_DONE, 0)

    def find(task):
        mine = task < own
        row = jnp.where(mine, 0, 3)
        lane = jnp.minimum(jnp.where(mine, OWN_DONE + task, SIDE_DONE + task - own), 127)
        place = pairs[row + 1, lane] + jnp.where(mine, 0, BOXES)
        return pairs[row, lane], place, jnp.where(task < tasks, pairs[row + 2, lane], 0)

    for load in loads:
        load.wait()

    def measure(task):
        box, place, _ = find(task)
        return squares(source[place], target[box])

    dist[0] = measure(0)

    def turn(n, carry):
        for k in range(TURN):
            task = n * TURN + k
            square = dist[k % 2]
            dist[1 - k % 2] = measure(task + 1)
            box, place, times = find(task)
            lanes = pl.ds(pl.multiple_of(box * POINTS, POINTS), POINTS)
            out[:, lanes] += (times.astype(F32) * SCALE) * dot(vec[place], tile_of(square))
        return carry

    lax.fori_loop(0, (tasks + TURN - 1) // TURN, turn, 0)


def near_field(total, pairs, *arrays):
    return pl.pallas_call(
        near_kernel,
        out_shape=jax.ShapeDtypeStruct((PROBES, WIDTH), F32),
        in_specs=[SMEM] + [HBM] * 6,
        out_specs=VMEM,
        scratch_shapes=[
            pltpu.VMEM((3 * BOXES, PROBES, POINTS), BF),
            pltpu.VMEM((3 * BOXES, PROBES, POINTS), BF),
            pltpu.VMEM((BOXES, PROBES, POINTS), BF),
            pltpu.VMEM((2, POINTS, POINTS), F32),
            pltpu.SemaphoreType.DMA((6,)),
        ],
        compiler_params=pltpu.CompilerParams(vmem_limit_bytes=VMEM_LIMIT),
    )(pairs, total, *arrays)


def local(gy_count, coords, vectors, *rest):
    matrices, near_list, near_count = rest[:-2], rest[-2], rest[-1]
    return near_field(*far_field(gy_count, coords, vectors, near_list, near_count, *matrices))


def solution(mesh):
    both = ("gx", "gy")
    return jax.shard_map(
        functools.partial(local, mesh.shape["gy"]),
        mesh=mesh,
        in_specs=(
            P(None, both),
            P(None, both),
            P(both, None, None),
            P(both, None, None),
            P(both, None, None),
            P("gx", None, None),
            P(both, None, None, None),
            P("gx", None, None, None),
            P("gx", None, None, None),
            P(both, None),
            P("gx", None),
            P("gx", None),
            P(both, None),
            P(both),
        ),
        out_specs=P(None, both),
        check_vma=False,
    )
```

```python
import functools
import math

import jax
import jax.numpy as jnp
from jax import lax
from jax.experimental import pallas as pl
from jax.experimental.pallas import tpu as pltpu
from jax.sharding import PartitionSpec as P

MESH = pl.DeviceIdType.MESH
F32 = jnp.float32
BF = jnp.bfloat16
I32 = jnp.int32
BOXES = 8
POINTS = 512
PROBES = 16
RANK = 128
NEAR = 16
FAR = 6
WIDTH = BOXES * POINTS
GX = 8
LINE = 16
LINES = 4
GROUP = 8
TURN = 4
OWN_TURNS = 7
MID_TURNS = 2
LAST_TURNS = 2
OWN_DONE = OWN_TURNS * TURN
SIDE_DONE = (MID_TURNS + LAST_TURNS) * TURN
SCALE = POINTS**-0.5
VMEM_LIMIT = 30 << 20
HBM = pl.BlockSpec(memory_space=pltpu.HBM)
ANY = pl.BlockSpec(memory_space=pl.ANY)
VMEM = pl.BlockSpec(memory_space=pltpu.VMEM)
SMEM = pl.BlockSpec(memory_space=pltpu.SMEM)


def dot(a, b):
    return jnp.dot(a, b, preferred_element_type=F32)


def dot_t(a, b):
    return lax.dot_general(a, b, (((1,), (1,)), ((), ())), preferred_element_type=F32)


def span(box):
    return slice(box * POINTS, (box + 1) * POINTS)


def gather(ref, index_of):
    return jnp.concatenate([ref[index_of(f)] for f in range(FAR)], axis=1)


def squares(source, target):
    return lax.dot_general(source, target, (((0,), (0,)), ((), ())), preferred_element_type=F32)


def tile_of(square):
    square = jnp.maximum(square, 1e-30)
    return jnp.exp2((square * -math.log2(math.e)) * lax.rsqrt(square)).astype(BF)


def norm_parts(parts):
    norm = parts[0] * parts[0] + parts[1] * parts[1] + parts[2] * parts[2]
    high = norm.astype(BF).astype(F32)
    rest = norm - high
    middle = rest.astype(BF).astype(F32)
    return [high, middle, rest - middle]


def set_rows(raw, first, values):
    for n, value in enumerate(values):
        for box in range(BOXES):
            raw[box, first + n : first + n + 1, :] = value[box : box + 1, :]


def compact(times, box, place):
    count = times.shape[0]
    across = lax.broadcasted_iota(I32, (count, 128), 1)
    down = lax.broadcasted_iota(I32, (count, 128), 0)
    live = jnp.broadcast_to(jnp.where(times > 0, 1, 0), (count, 128))
    along = jnp.sum(jnp.where(across == down, live, 0), axis=0, keepdims=True)
    rank = jnp.sum(jnp.where(across < down, along, 0), axis=1, keepdims=True)
    hit = (rank == across) & (live > 0)
    rows = [jnp.sum(jnp.where(hit, value, 0), axis=0, keepdims=True) for value in (box, place, times)]
    return rows, jnp.sum(live, axis=0, keepdims=True)


def pair_lists(near_list, near_count, gy, gy_count, out):
    place = lax.broadcasted_iota(I32, (3 * BOXES, NEAR), 0)
    slot = lax.broadcasted_iota(I32, (3 * BOXES, NEAR), 1)
    column = gy + place // BOXES - 1
    inside = (column >= 0) & (column < gy_count)
    own, side = [], []
    for box in range(BOXES):
        named = (near_list[box : box + 1, :] == place) & (slot < near_count[box]) & inside
        times = jnp.sum(jnp.where(named, 1, 0), axis=1, keepdims=True)
        own.append(times[BOXES : 2 * BOXES])
        side += [times[:BOXES], times[2 * BOXES :]]
    own, side = jnp.concatenate(own, axis=0), jnp.concatenate(side, axis=0)
    n = lax.broadcasted_iota(I32, own.shape, 0)
    own_rows, own_count = compact(own, n // BOXES, n % BOXES)
    n = lax.broadcasted_iota(I32, side.shape, 0)
    side_rows, side_count = compact(side, n // (2 * BOXES), n % (2 * BOXES))
    for n, row in enumerate(own_rows + side_rows + [own_count, side_count]):
        out[n : n + 1, :] = row


def far_kernel(
    gy_count,
    coords_hbm,
    vectors_hbm,
    list_hbm,
    count_hbm,
    basis_hbm,
    leaf_hbm,
    mid_hbm,
    top_hbm,
    one_hbm,
    two_hbm,
    three_hbm,
    far_one_hbm,
    far_two_hbm,
    far_three_hbm,
    total,
    pairs,
    own_vec_out,
    side_vec_out,
    own_source_out,
    side_source_out,
    target_out,
    own_vec,
    side_vec,
    own_source,
    side_source,
    target,
    coords,
    vectors,
    near_list,
    near_count,
    basis,
    leaf_up,
    mid_up,
    top_up,
    couple_one,
    couple_two,
    couple_three,
    far_one,
    far_two,
    far_three,
    pos_f32,
    pos,
    side_pos,
    raw,
    dist,
    tasks,
    down_three,
    down_leaf,
    toward,
    level_two,
    level_three,
    row_one,
    load_sem,
    task_sem,
    out_sem,
    side_send,
    side_recv,
    toward_send,
    toward_recv,
    line_send,
    line_recv,
    two_send,
    two_recv,
    row_send,
    row_recv,
    three_send,
    three_recv,
):
    gx = lax.axis_index("gx")
    gy = lax.axis_index("gy")
    x = gy // LINE
    z = gy % LINE
    group = gy // GROUP
    loads = [
        pltpu.make_async_copy(source, goal, load_sem.at[n])
        for n, (source, goal) in enumerate(
            (
                (vectors_hbm, vectors),
                (coords_hbm, coords),
                (list_hbm, near_list),
                (count_hbm, near_count),
                (basis_hbm, basis),
                (leaf_hbm, leaf_up),
                (mid_hbm, mid_up),
                (top_hbm, top_up),
                (two_hbm.at[group], couple_two),
                (three_hbm, couple_three),
                (one_hbm, couple_one),
                (far_one_hbm, far_one),
                (far_two_hbm, far_two),
                (far_three_hbm, far_three),
            )
        )
    ]
    for load in loads:
        load.start()

    right = (gy + 1) % gy_count
    left = (gy + gy_count - 1) % gy_count

    def in_line(step):
        return x * LINE + (z + step) % LINE

    def in_plane(step):
        return ((x + step) % LINES) * LINE + z

    barrier = pltpu.get_barrier_semaphore()

    def greet(peer):
        pl.semaphore_signal(barrier, inc=1, device_id=peer, device_id_type=MESH)

    def greet_line(n, carry):
        greet((gx, in_line(n)))
        return carry

    def greet_three(n, carry):
        greet(((gx + n) % GX, gy))
        return carry

    lax.fori_loop(1, LINE, greet_line, 0)
    for n in range(1, LINES):
        greet((gx, in_plane(n)))
    lax.fori_loop(1, GX, greet_three, 0)
    greet((gx, left))
    greet((gx, right))

    loads[0].wait()
    for box in range(BOXES):
        own_vec[box] = vectors[:, span(box)].astype(BF)
    loads[4].wait()
    loads[5].wait()
    leaf = jnp.concatenate([dot(own_vec[b], basis[b]).astype(BF) for b in range(BOXES)], axis=1)
    ups = leaf_up[...].reshape(BOXES * RANK, RANK)
    one = dot(leaf, ups).astype(BF)
    row_one[gy] = one
    loads[6].wait()
    toward[z] = dot(one, mid_up[0]).astype(BF)

    loads[1].wait()
    for comp in range(3):
        for box in range(BOXES):
            row = comp * BOXES + box
            pos_f32[row : row + 1, :] = coords[comp : comp + 1, span(box)].astype(F32)
    pos_f32[24:32, :] = jnp.zeros((8, POINTS), F32)
    pos[...] = pos_f32[...].astype(BF)
    def send(ref, sends, recvs, step, slot, peer):
        return pltpu.make_async_remote_copy(
            src_ref=ref,
            dst_ref=ref,
            send_sem=sends.at[step],
            recv_sem=recvs.at[slot],
            device_id=peer,
            device_id_type=MESH,
        )

    def toward_copy(step, slot):
        return send(toward.at[z], toward_send, toward_recv, step, slot, (gx, in_line(step)))

    def line_copy(step, slot):
        return send(row_one.at[gy], line_send, line_recv, step, slot, (gx, in_line(step)))

    def two_copy(step, slot):
        return send(level_two.at[x], two_send, two_recv, step, slot, (gx, in_plane(step)))

    def row_copy(step, slot):
        part = row_one.at[pl.ds(x * LINE, LINE)]
        return send(part, row_send, row_recv, step, slot, (gx, in_plane(step)))

    def three_copy(step, slot):
        return send(level_three.at[gx], three_send, three_recv, step, slot, ((gx + step) % GX, gy))

    def each(count, do):
        def body(n, carry):
            do(n)
            return carry

        lax.fori_loop(1, count, body, 0)

    def start_all(copy, mine, count):
        each(count, lambda n: copy(n, mine).start())

    def start_far_first(copy, mine):
        for n in (8, 7, 9, 6, 10, 5, 11, 4, 12, 3, 13, 2, 14, 1, 15):
            copy(n, mine).start()

    def arrive_all(copy, mine, count):
        each(count, lambda n: copy(n, (mine + n) % count).wait_recv())

    def sent_all(copy, mine, count):
        each(count, lambda n: copy(n, mine).wait_send())

    sides = []
    for n, (source, goal, rows) in enumerate(((own_vec, side_vec, 8), (pos, side_pos, 32))):
        for side, peer in ((0, right), (1, left)):
            sides.append(
                pltpu.make_async_remote_copy(
                    src_ref=source,
                    dst_ref=goal.at[pl.ds(side * rows, rows)],
                    send_sem=side_send.at[2 * n + side],
                    recv_sem=side_recv.at[2 * n + side],
                    device_id=(gx, peer),
                    device_id_type=MESH,
                )
            )

    def enter():
        pl.semaphore_wait(barrier, LINE - 1 + LINES - 1 + GX - 1 + 2)
        start_far_first(toward_copy, z)
        start_far_first(line_copy, z)
        for copy in sides:
            copy.start()

    late = (z // 8) * (1 - z // 12)
    ahead = (1 - z // 8) * (OWN_TURNS - z // 2) + z // 14

    pl.when(late == 1)(enter)

    loads[2].wait()
    loads[3].wait()
    pair_lists(near_list, near_count, gy, gy_count, pairs)
    task_copy = pltpu.make_async_copy(pairs, tasks, task_sem.at[0])
    task_copy.start()

    raw[...] = jnp.zeros_like(raw)
    ones = [jnp.ones((BOXES, POINTS), F32)] * 3
    parts = [pos_f32[n * BOXES : (n + 1) * BOXES, :] for n in range(3)]
    norms = norm_parts(parts)
    set_rows(raw, 0, parts + ones + norms)
    target[...] = raw[...].astype(BF)
    set_rows(raw, 0, [-2.0 * part for part in parts] + norms + ones)
    own_source[...] = raw[...].astype(BF)
    outs = [
        pltpu.make_async_copy(source, goal, out_sem.at[n])
        for n, (source, goal) in enumerate(
            (
                (own_vec, own_vec_out),
                (own_source, own_source_out),
                (target, target_out),
                (side_vec, side_vec_out),
                (side_source, side_source_out),
            )
        )
    ]
    for copy in outs[:3]:
        copy.start()
    total[...] = jnp.zeros_like(total)
    task_copy.wait()

    def begin(first_row, source_ref, task):
        dist[0] = squares(source_ref[tasks[first_row + 1, task]], target[tasks[first_row, task]])

    def fill(first_row, source_ref, vec_ref, first, last):
        def turn(n, carry):
            for k in range(TURN):
                task = n * TURN + k
                square = dist[k % 2]
                dist[1 - k % 2] = squares(
                    source_ref[tasks[first_row + 1, task + 1]], target[tasks[first_row, task + 1]]
                )
                part = dot(vec_ref[tasks[first_row + 1, task]], tile_of(square))
                box = tasks[first_row, task]
                weight = tasks[first_row + 2, task].astype(F32) * SCALE
                for b in range(BOXES):
                    total[:, span(b)] += jnp.where(box == b, weight, 0.0) * part
            return carry

        lax.fori_loop(first, last, turn, 0)

    begin(0, own_source, 0)
    fill(0, own_source, own_vec, 0, ahead)

    pl.when(late == 0)(enter)

    fill(0, own_source, own_vec, ahead, OWN_TURNS)

    for load in loads[7:]:
        load.wait()
    down = dot(mid_up[0], top_up[group]).astype(BF)
    down_three[...] = dot_t(couple_three[0].reshape(FAR * RANK, RANK), down).astype(BF)
    for b in range(BOXES):
        down_leaf[b * POINTS : (b + 1) * POINTS, :] = dot(basis[b], leaf_up[b]).astype(BF)

    arrive_all(toward_copy, z, LINE)
    for half in range(2):
        two = jnp.zeros((PROBES, RANK), F32)
        for n in range(GROUP):
            two = two + toward[half * GROUP + n].astype(F32)
        level_two[x, half] = two.astype(BF)
    start_all(two_copy, x, LINES)
    arrive_all(line_copy, z, LINE)
    start_all(row_copy, x, LINES)

    for copy in sides:
        copy.wait_recv()
    for side in range(2):
        first = side * 32
        near = side_pos[first : first + 24, :].astype(F32)
        parts = [near[n * BOXES : (n + 1) * BOXES, :] for n in range(3)]
        set_rows(raw, 0, [-2.0 * part for part in parts] + norm_parts(parts))
        side_source[side * BOXES : (side + 1) * BOXES] = raw[...].astype(BF)
    for copy in outs[3:]:
        copy.start()
    begin(3, side_source, 0)
    fill(3, side_source, side_vec, 0, MID_TURNS)

    arrive_all(two_copy, x, LINES)
    twos = jnp.concatenate([level_two[n // 2, n % 2] for n in range(8)], axis=1)
    level_three[gx] = dot(twos, top_up[...].reshape(8 * RANK, RANK)).astype(BF)
    start_all(three_copy, gx, GX)

    source_two = gather(level_two, lambda f: (far_two[group, f] // 2, far_two[group, f] % 2))
    local_two = dot(source_two, couple_two[...].reshape(FAR * RANK, RANK))
    local_one = dot_t(local_two.astype(BF), mid_up[0])
    fill(3, side_source, side_vec, MID_TURNS, MID_TURNS + LAST_TURNS)

    arrive_all(row_copy, x, LINES)
    local_one = local_one + dot(
        gather(row_one, lambda f: far_one[0, f]), couple_one[0].reshape(FAR * RANK, RANK)
    )
    arrive_all(three_copy, gx, GX)
    local_one = local_one + dot(gather(level_three, lambda f: far_three[0, f]), down_three[...])
    total[...] += dot_t(local_one.astype(BF), down_leaf[...])

    for copy in outs:
        copy.wait()
    for copy in sides:
        copy.wait_send()
    sent_all(toward_copy, z, LINE)
    sent_all(line_copy, z, LINE)
    sent_all(two_copy, x, LINES)
    sent_all(row_copy, x, LINES)
    sent_all(three_copy, gx, GX)


def far_field(gy_count, *arrays):
    dma = pltpu.SemaphoreType.DMA
    boxes = (BOXES, PROBES, POINTS)
    sides = (2 * BOXES, PROBES, POINTS)
    return pl.pallas_call(
        functools.partial(far_kernel, gy_count),
        out_shape=(
            jax.ShapeDtypeStruct((PROBES, WIDTH), F32),
            jax.ShapeDtypeStruct((8, 128), I32),
            jax.ShapeDtypeStruct(boxes, BF),
            jax.ShapeDtypeStruct(sides, BF),
            jax.ShapeDtypeStruct(boxes, BF),
            jax.ShapeDtypeStruct(sides, BF),
            jax.ShapeDtypeStruct(boxes, BF),
        ),
        in_specs=[HBM] * 14,
        out_specs=(VMEM, VMEM) + (ANY,) * 5,
        scratch_shapes=[
            pltpu.VMEM(boxes, BF),
            pltpu.VMEM(sides, BF),
            pltpu.VMEM(boxes, BF),
            pltpu.VMEM(sides, BF),
            pltpu.VMEM(boxes, BF),
            pltpu.VMEM((3, WIDTH), BF),
            pltpu.VMEM((PROBES, WIDTH), F32),
            pltpu.VMEM((BOXES, NEAR), I32),
            pltpu.SMEM((BOXES,), I32),
            pltpu.VMEM((BOXES, POINTS, RANK), BF),
            pltpu.VMEM((BOXES, RANK, RANK), BF),
            pltpu.VMEM((1, RANK, RANK), BF),
            pltpu.VMEM((8, RANK, RANK), BF),
            pltpu.VMEM((1, FAR, RANK, RANK), BF),
            pltpu.VMEM((FAR, RANK, RANK), BF),
            pltpu.VMEM((1, FAR, RANK, RANK), BF),
            pltpu.SMEM((1, FAR), I32),
            pltpu.SMEM((8, FAR), I32),
            pltpu.SMEM((1, FAR), I32),
            pltpu.VMEM((32, POINTS), F32),
            pltpu.VMEM((32, POINTS), BF),
            pltpu.VMEM((64, POINTS), BF),
            pltpu.VMEM(boxes, F32),
            pltpu.VMEM((2, POINTS, POINTS), F32),
            pltpu.SMEM((8, 128), I32),
            pltpu.VMEM((FAR * RANK, RANK), BF),
            pltpu.VMEM((WIDTH, RANK), BF),
            pltpu.VMEM((LINE, PROBES, RANK), BF),
            pltpu.VMEM((LINES, 2, PROBES, RANK), BF),
            pltpu.VMEM((GX, PROBES, RANK), BF),
            pltpu.VMEM((LINE * LINES, PROBES, RANK), BF),
            dma((14,)),
            dma((1,)),
            dma((5,)),
            dma((4,)),
            dma((4,)),
            dma((LINE,)),
            dma((LINE,)),
            dma((LINE,)),
            dma((LINE,)),
            dma((LINES,)),
            dma((LINES,)),
            dma((LINES,)),
            dma((LINES,)),
            dma((GX,)),
            dma((GX,)),
        ],
        compiler_params=pltpu.CompilerParams(
            collective_id=0, has_side_effects=True, vmem_limit_bytes=VMEM_LIMIT
        ),
    )(*arrays)


def near_kernel(pairs_hbm, total_hbm, own_vec, side_vec, own_source, side_source, target_hbm, out, pairs, vec, source, target, dist, sem):
    loads = [
        pltpu.make_async_copy(a, b, sem.at[n])
        for n, (a, b) in enumerate(
            (
                (pairs_hbm, pairs),
                (own_source, source.at[pl.ds(0, BOXES)]),
                (side_source, source.at[pl.ds(BOXES, 2 * BOXES)]),
                (target_hbm, target),
                (own_vec, vec.at[pl.ds(0, BOXES)]),
                (side_vec, vec.at[pl.ds(BOXES, 2 * BOXES)]),
                (total_hbm, out),
            )
        )
    ]
    for load in loads:
        load.start()
    loads[0].wait()
    own = jnp.maximum(pairs[6, 0] - OWN_DONE, 0)
    tasks = own + jnp.maximum(pairs[7, 0] - SIDE_DONE, 0)

    def find(task):
        mine = task < own
        row = jnp.where(mine, 0, 3)
        lane = jnp.minimum(jnp.where(mine, OWN_DONE + task, SIDE_DONE + task - own), 127)
        place = pairs[row + 1, lane] + jnp.where(mine, 0, BOXES)
        return pairs[row, lane], place, jnp.where(task < tasks, pairs[row + 2, lane], 0)

    for load in loads[1:]:
        load.wait()

    def measure(task):
        box, place, _ = find(task)
        return squares(source[place], target[box])

    dist[0] = measure(0)

    def turn(n, carry):
        for k in range(TURN):
            task = n * TURN + k
            square = dist[k % 2]
            dist[1 - k % 2] = measure(task + 1)
            box, place, times = find(task)
            lanes = pl.ds(pl.multiple_of(box * POINTS, POINTS), POINTS)
            out[:, lanes] += (times.astype(F32) * SCALE) * dot(vec[place], tile_of(square))
        return carry

    lax.fori_loop(0, (tasks + TURN - 1) // TURN, turn, 0)


def near_field(total, pairs, *arrays):
    return pl.pallas_call(
        near_kernel,
        out_shape=jax.ShapeDtypeStruct((PROBES, WIDTH), F32),
        in_specs=[ANY] * 7,
        out_specs=VMEM,
        scratch_shapes=[
            pltpu.SMEM((8, 128), I32),
            pltpu.VMEM((3 * BOXES, PROBES, POINTS), BF),
            pltpu.VMEM((3 * BOXES, PROBES, POINTS), BF),
            pltpu.VMEM((BOXES, PROBES, POINTS), BF),
            pltpu.VMEM((2, POINTS, POINTS), F32),
            pltpu.SemaphoreType.DMA((7,)),
        ],
        compiler_params=pltpu.CompilerParams(vmem_limit_bytes=VMEM_LIMIT),
    )(pairs, total, *arrays)


def local(gy_count, coords, vectors, *rest):
    matrices, near_list, near_count = rest[:-2], rest[-2], rest[-1]
    arrays = (coords, vectors, near_list, near_count, *matrices)
    return near_field(*far_field(gy_count, *(pltpu.with_memory_space_constraint(a, pltpu.HBM) for a in arrays)))


def solution(mesh):
    both = ("gx", "gy")
    return jax.shard_map(
        functools.partial(local, mesh.shape["gy"]),
        mesh=mesh,
        in_specs=(
            P(None, both),
            P(None, both),
            P(both, None, None),
            P(both, None, None),
            P(both, None, None),
            P("gx", None, None),
            P(both, None, None, None),
            P("gx", None, None, None),
            P("gx", None, None, None),
            P(both, None),
            P("gx", None),
            P("gx", None),
            P(both, None),
            P(both),
        ),
        out_specs=P(None, both),
        check_vma=False,
    )
```

```python
import functools
import math

import jax
import jax.numpy as jnp
from jax import lax
from jax.experimental import pallas as pl
from jax.experimental.pallas import tpu as pltpu
from jax.sharding import PartitionSpec as P

MESH = pl.DeviceIdType.MESH
F32 = jnp.float32
BF = jnp.bfloat16
I32 = jnp.int32
BOXES = 8
POINTS = 512
PROBES = 16
RANK = 128
NEAR = 16
FAR = 6
WIDTH = BOXES * POINTS
GX = 8
LINE = 16
LINES = 4
GROUP = 8
TURN = 6
OWN_TURNS = 5
MID_TURNS = 1
LAST_TURNS = 3
OWN_DONE = OWN_TURNS * TURN
SIDE_DONE = (MID_TURNS + LAST_TURNS) * TURN
SCALE = POINTS**-0.5
VMEM_LIMIT = 30 << 20
HBM = pl.BlockSpec(memory_space=pltpu.HBM)
ANY = pl.BlockSpec(memory_space=pl.ANY)
VMEM = pl.BlockSpec(memory_space=pltpu.VMEM)
SMEM = pl.BlockSpec(memory_space=pltpu.SMEM)


def dot(a, b):
    return jnp.dot(a, b, preferred_element_type=F32)


def dot_t(a, b):
    return lax.dot_general(a, b, (((1,), (1,)), ((), ())), preferred_element_type=F32)


def span(box):
    return slice(box * POINTS, (box + 1) * POINTS)


def gather(ref, index_of):
    return jnp.concatenate([ref[index_of(f)] for f in range(FAR)], axis=1)


def squares(source, target):
    return lax.dot_general(source, target, (((0,), (0,)), ((), ())), preferred_element_type=F32)


def tile_of(square):
    square = jnp.maximum(square, 1e-30)
    return jnp.exp2((square * -math.log2(math.e)) * lax.rsqrt(square)).astype(BF)


def norm_parts(parts):
    norm = parts[0] * parts[0] + parts[1] * parts[1] + parts[2] * parts[2]
    high = norm.astype(BF).astype(F32)
    rest = norm - high
    middle = rest.astype(BF).astype(F32)
    return [high, middle, rest - middle]


def set_rows(raw, first, values):
    for n, value in enumerate(values):
        for box in range(BOXES):
            raw[box, first + n : first + n + 1, :] = value[box : box + 1, :]


def compact(times, box, place):
    count = times.shape[0]
    across = lax.broadcasted_iota(I32, (count, 128), 1)
    down = lax.broadcasted_iota(I32, (count, 128), 0)
    live = jnp.broadcast_to(jnp.where(times > 0, 1, 0), (count, 128))
    along = jnp.sum(jnp.where(across == down, live, 0), axis=0, keepdims=True)
    rank = jnp.sum(jnp.where(across < down, along, 0), axis=1, keepdims=True)
    hit = (rank == across) & (live > 0)
    rows = [jnp.sum(jnp.where(hit, value, 0), axis=0, keepdims=True) for value in (box, place, times)]
    return rows, jnp.sum(live, axis=0, keepdims=True)


def pair_lists(near_list, near_count, gy, gy_count, out):
    place = lax.broadcasted_iota(I32, (3 * BOXES, NEAR), 0)
    slot = lax.broadcasted_iota(I32, (3 * BOXES, NEAR), 1)
    column = gy + place // BOXES - 1
    inside = (column >= 0) & (column < gy_count)
    own, side = [], []
    for box in range(BOXES):
        named = (near_list[box : box + 1, :] == place) & (slot < near_count[box]) & inside
        times = jnp.sum(jnp.where(named, 1, 0), axis=1, keepdims=True)
        own.append(times[BOXES : 2 * BOXES])
        side += [times[:BOXES], times[2 * BOXES :]]
    own, side = jnp.concatenate(own, axis=0), jnp.concatenate(side, axis=0)
    n = lax.broadcasted_iota(I32, own.shape, 0)
    own_rows, own_count = compact(own, n // BOXES, n % BOXES)
    n = lax.broadcasted_iota(I32, side.shape, 0)
    side_rows, side_count = compact(side, n // (2 * BOXES), n % (2 * BOXES))
    for n, row in enumerate(own_rows + side_rows + [own_count, side_count]):
        out[n : n + 1, :] = row


def far_kernel(
    gy_count,
    coords_hbm,
    vectors_hbm,
    list_hbm,
    count_hbm,
    basis_hbm,
    leaf_hbm,
    mid_hbm,
    top_hbm,
    one_hbm,
    two_hbm,
    three_hbm,
    far_one_hbm,
    far_two_hbm,
    far_three_hbm,
    total,
    pairs,
    own_vec_out,
    side_vec_out,
    own_source_out,
    side_source_out,
    target_out,
    own_vec,
    side_vec,
    own_source,
    side_source,
    target,
    coords,
    vectors,
    near_list,
    near_count,
    basis,
    leaf_up,
    mid_up,
    top_up,
    couple_one,
    couple_two,
    couple_three,
    far_one,
    far_two,
    far_three,
    pos_f32,
    pos,
    side_pos,
    raw,
    dist,
    tasks,
    down_three,
    down_leaf,
    toward,
    level_two,
    level_three,
    row_one,
    load_sem,
    task_sem,
    out_sem,
    side_send,
    side_recv,
    toward_send,
    toward_recv,
    line_send,
    line_recv,
    two_send,
    two_recv,
    row_send,
    row_recv,
    three_send,
    three_recv,
):
    gx = lax.axis_index("gx")
    gy = lax.axis_index("gy")
    x = gy // LINE
    z = gy % LINE
    group = gy // GROUP
    loads = [
        pltpu.make_async_copy(source, goal, load_sem.at[n])
        for n, (source, goal) in enumerate(
            (
                (vectors_hbm, vectors),
                (coords_hbm, coords),
                (list_hbm, near_list),
                (count_hbm, near_count),
                (basis_hbm, basis),
                (leaf_hbm, leaf_up),
                (mid_hbm, mid_up),
                (top_hbm, top_up),
                (two_hbm.at[group], couple_two),
                (three_hbm, couple_three),
                (one_hbm, couple_one),
                (far_one_hbm, far_one),
                (far_two_hbm, far_two),
                (far_three_hbm, far_three),
            )
        )
    ]
    for n in (0, 1, 4, 5, 6):
        loads[n].start()

    right = (gy + 1) % gy_count
    left = (gy + gy_count - 1) % gy_count

    def in_line(step):
        return x * LINE + (z + step) % LINE

    def in_plane(step):
        return ((x + step) % LINES) * LINE + z

    barrier = pltpu.get_barrier_semaphore()

    def greet(peer):
        pl.semaphore_signal(barrier, inc=1, device_id=peer, device_id_type=MESH)

    def greet_line(n, carry):
        greet((gx, in_line(n)))
        return carry

    def greet_three(n, carry):
        greet(((gx + n) % GX, gy))
        return carry

    lax.fori_loop(1, LINE, greet_line, 0)
    for n in range(1, LINES):
        greet((gx, in_plane(n)))
    lax.fori_loop(1, GX, greet_three, 0)
    greet((gx, left))
    greet((gx, right))
    for n in (2, 3, *range(7, 14)):
        loads[n].start()

    loads[1].wait()
    for comp in range(3):
        for box in range(BOXES):
            row = comp * BOXES + box
            pos_f32[row : row + 1, :] = coords[comp : comp + 1, span(box)].astype(F32)
    pos_f32[24:32, :] = jnp.zeros((8, POINTS), F32)
    pos[...] = pos_f32[...].astype(BF)

    loads[0].wait()
    for box in range(BOXES):
        own_vec[box] = vectors[:, span(box)].astype(BF)
    loads[4].wait()
    loads[5].wait()
    leaf = jnp.concatenate([dot(own_vec[b], basis[b]).astype(BF) for b in range(BOXES)], axis=1)
    ups = leaf_up[...].reshape(BOXES * RANK, RANK)
    one = dot(leaf, ups).astype(BF)
    row_one[gy] = one
    loads[6].wait()
    toward[z] = dot(one, mid_up[0]).astype(BF)

    def send(ref, sends, recvs, step, slot, peer):
        return pltpu.make_async_remote_copy(
            src_ref=ref,
            dst_ref=ref,
            send_sem=sends.at[step],
            recv_sem=recvs.at[slot],
            device_id=peer,
            device_id_type=MESH,
        )

    def toward_copy(step, slot):
        return send(toward.at[z], toward_send, toward_recv, step, slot, (gx, in_line(step)))

    def line_copy(step, slot):
        return send(row_one.at[gy], line_send, line_recv, step, slot, (gx, in_line(step)))

    def two_copy(step, slot):
        return send(level_two.at[x], two_send, two_recv, step, slot, (gx, in_plane(step)))

    def row_copy(step, slot):
        part = row_one.at[pl.ds(x * LINE, LINE)]
        return send(part, row_send, row_recv, step, slot, (gx, in_plane(step)))

    def three_copy(step, slot):
        return send(level_three.at[gx], three_send, three_recv, step, slot, ((gx + step) % GX, gy))

    def each(count, do):
        def body(n, carry):
            do(n)
            return carry

        lax.fori_loop(1, count, body, 0)

    def start_all(copy, mine, count):
        each(count, lambda n: copy(n, mine).start())

    def start_far_first(copy, mine):
        for n in (8, 7, 9, 6, 10, 5, 11, 4, 12, 3, 13, 2, 14, 1, 15):
            copy(n, mine).start()

    def arrive_all(copy, mine, count):
        each(count, lambda n: copy(n, (mine + n) % count).wait_recv())

    def sent_all(copy, mine, count):
        each(count, lambda n: copy(n, mine).wait_send())

    sides = []
    for n, (source, goal, rows) in enumerate(((own_vec, side_vec, 8), (pos, side_pos, 32))):
        for side, peer in ((0, right), (1, left)):
            sides.append(
                pltpu.make_async_remote_copy(
                    src_ref=source,
                    dst_ref=goal.at[pl.ds(side * rows, rows)],
                    send_sem=side_send.at[2 * n + side],
                    recv_sem=side_recv.at[2 * n + side],
                    device_id=(gx, peer),
                    device_id_type=MESH,
                )
            )

    def enter():
        pl.semaphore_wait(barrier, LINE - 1 + LINES - 1 + GX - 1 + 2)
        start_far_first(toward_copy, z)
        for copy in sides:
            copy.start()
        start_far_first(line_copy, z)

    late = (z // 8) * (1 - z // 12)
    ahead = (1 - z // 8) * (OWN_TURNS - (z // 4) * (z // 2 - 1)) + z // 12

    pl.when(late == 1)(enter)

    raw[...] = jnp.zeros_like(raw)
    ones = [jnp.ones((BOXES, POINTS), F32)] * 3
    parts = [pos_f32[n * BOXES : (n + 1) * BOXES, :] for n in range(3)]
    norms = norm_parts(parts)
    set_rows(raw, 0, parts + ones + norms)
    target[...] = raw[...].astype(BF)
    set_rows(raw, 0, [-2.0 * part for part in parts] + norms + ones)
    own_source[...] = raw[...].astype(BF)
    outs = [
        pltpu.make_async_copy(source, goal, out_sem.at[n])
        for n, (source, goal) in enumerate(
            (
                (own_vec, own_vec_out),
                (own_source, own_source_out),
                (target, target_out),
                (side_vec, side_vec_out),
                (side_source, side_source_out),
            )
        )
    ]
    for copy in outs[:3]:
        copy.start()
    total[...] = jnp.zeros_like(total)
    loads[2].wait()
    loads[3].wait()
    pair_lists(near_list, near_count, gy, gy_count, pairs)
    task_copy = pltpu.make_async_copy(pairs, tasks, task_sem.at[0])
    task_copy.start()

    task_copy.wait()

    def begin(first_row, source_ref, task):
        dist[0] = squares(source_ref[tasks[first_row + 1, task]], target[tasks[first_row, task]])

    def fill(first_row, source_ref, vec_ref, first, last):
        def turn(n, carry):
            for k in range(TURN):
                task = n * TURN + k
                square = dist[k % 2]
                dist[1 - k % 2] = squares(
                    source_ref[tasks[first_row + 1, task + 1]], target[tasks[first_row, task + 1]]
                )
                part = dot(vec_ref[tasks[first_row + 1, task]], tile_of(square))
                box = tasks[first_row, task]
                weight = tasks[first_row + 2, task].astype(F32) * SCALE
                for b in range(BOXES):
                    total[:, span(b)] += jnp.where(box == b, weight, 0.0) * part
            return carry

        lax.fori_loop(first, last, turn, 0)

    begin(0, own_source, 0)
    fill(0, own_source, own_vec, 0, ahead)

    pl.when(late == 0)(enter)

    fill(0, own_source, own_vec, ahead, OWN_TURNS)

    for load in loads[7:]:
        load.wait()
    down = dot(mid_up[0], top_up[group]).astype(BF)
    down_three[...] = dot_t(couple_three[0].reshape(FAR * RANK, RANK), down).astype(BF)
    for b in range(BOXES):
        down_leaf[b * POINTS : (b + 1) * POINTS, :] = dot(basis[b], leaf_up[b]).astype(BF)

    arrive_all(toward_copy, z, LINE)
    for half in range(2):
        two = jnp.zeros((PROBES, RANK), F32)
        for n in range(GROUP):
            two = two + toward[half * GROUP + n].astype(F32)
        level_two[x, half] = two.astype(BF)
    start_all(two_copy, x, LINES)
    for copy in sides:
        copy.wait_recv()
    for side in range(2):
        first = side * 32
        near = side_pos[first : first + 24, :].astype(F32)
        parts = [near[n * BOXES : (n + 1) * BOXES, :] for n in range(3)]
        set_rows(raw, 0, [-2.0 * part for part in parts] + norm_parts(parts))
        side_source[side * BOXES : (side + 1) * BOXES] = raw[...].astype(BF)
    for copy in outs[3:]:
        copy.start()
    begin(3, side_source, 0)
    fill(3, side_source, side_vec, 0, MID_TURNS)

    arrive_all(two_copy, x, LINES)
    twos = jnp.concatenate([level_two[n // 2, n % 2] for n in range(8)], axis=1)
    level_three[gx] = dot(twos, top_up[...].reshape(8 * RANK, RANK)).astype(BF)
    start_all(three_copy, gx, GX)
    arrive_all(line_copy, z, LINE)
    start_all(row_copy, x, LINES)

    source_two = gather(level_two, lambda f: (far_two[group, f] // 2, far_two[group, f] % 2))
    local_two = dot(source_two, couple_two[...].reshape(FAR * RANK, RANK))
    local_one = dot_t(local_two.astype(BF), mid_up[0])
    fill(3, side_source, side_vec, MID_TURNS, MID_TURNS + LAST_TURNS)

    arrive_all(three_copy, gx, GX)
    local_one = local_one + dot(gather(level_three, lambda f: far_three[0, f]), down_three[...])
    arrive_all(row_copy, x, LINES)
    local_one = local_one + dot(
        gather(row_one, lambda f: far_one[0, f]), couple_one[0].reshape(FAR * RANK, RANK)
    )
    total[...] += dot_t(local_one.astype(BF), down_leaf[...])

    for copy in outs:
        copy.wait()
    for copy in sides:
        copy.wait_send()
    sent_all(toward_copy, z, LINE)
    sent_all(line_copy, z, LINE)
    sent_all(two_copy, x, LINES)
    sent_all(row_copy, x, LINES)
    sent_all(three_copy, gx, GX)


def far_field(gy_count, *arrays):
    dma = pltpu.SemaphoreType.DMA
    boxes = (BOXES, PROBES, POINTS)
    sides = (2 * BOXES, PROBES, POINTS)
    return pl.pallas_call(
        functools.partial(far_kernel, gy_count),
        out_shape=(
            jax.ShapeDtypeStruct((PROBES, WIDTH), F32),
            jax.ShapeDtypeStruct((8, 128), I32),
            jax.ShapeDtypeStruct(boxes, BF),
            jax.ShapeDtypeStruct(sides, BF),
            jax.ShapeDtypeStruct(boxes, BF),
            jax.ShapeDtypeStruct(sides, BF),
            jax.ShapeDtypeStruct(boxes, BF),
        ),
        in_specs=[HBM] * 14,
        out_specs=(VMEM, VMEM) + (ANY,) * 5,
        scratch_shapes=[
            pltpu.VMEM(boxes, BF),
            pltpu.VMEM(sides, BF),
            pltpu.VMEM(boxes, BF),
            pltpu.VMEM(sides, BF),
            pltpu.VMEM(boxes, BF),
            pltpu.VMEM((3, WIDTH), BF),
            pltpu.VMEM((PROBES, WIDTH), F32),
            pltpu.VMEM((BOXES, NEAR), I32),
            pltpu.SMEM((BOXES,), I32),
            pltpu.VMEM((BOXES, POINTS, RANK), BF),
            pltpu.VMEM((BOXES, RANK, RANK), BF),
            pltpu.VMEM((1, RANK, RANK), BF),
            pltpu.VMEM((8, RANK, RANK), BF),
            pltpu.VMEM((1, FAR, RANK, RANK), BF),
            pltpu.VMEM((FAR, RANK, RANK), BF),
            pltpu.VMEM((1, FAR, RANK, RANK), BF),
            pltpu.SMEM((1, FAR), I32),
            pltpu.SMEM((8, FAR), I32),
            pltpu.SMEM((1, FAR), I32),
            pltpu.VMEM((32, POINTS), F32),
            pltpu.VMEM((32, POINTS), BF),
            pltpu.VMEM((64, POINTS), BF),
            pltpu.VMEM(boxes, F32),
            pltpu.VMEM((2, POINTS, POINTS), F32),
            pltpu.SMEM((8, 128), I32),
            pltpu.VMEM((FAR * RANK, RANK), BF),
            pltpu.VMEM((WIDTH, RANK), BF),
            pltpu.VMEM((LINE, PROBES, RANK), BF),
            pltpu.VMEM((LINES, 2, PROBES, RANK), BF),
            pltpu.VMEM((GX, PROBES, RANK), BF),
            pltpu.VMEM((LINE * LINES, PROBES, RANK), BF),
            dma((14,)),
            dma((1,)),
            dma((5,)),
            dma((4,)),
            dma((4,)),
            dma((LINE,)),
            dma((LINE,)),
            dma((LINE,)),
            dma((LINE,)),
            dma((LINES,)),
            dma((LINES,)),
            dma((LINES,)),
            dma((LINES,)),
            dma((GX,)),
            dma((GX,)),
        ],
        compiler_params=pltpu.CompilerParams(
            collective_id=0, has_side_effects=True, vmem_limit_bytes=VMEM_LIMIT
        ),
    )(*arrays)


def near_kernel(pairs_hbm, total, own_vec, side_vec, own_source, side_source, target, out, pairs, dist, sem):
    load = pltpu.make_async_copy(pairs_hbm, pairs, sem.at[0])
    load.start()
    out[...] = total[...]
    load.wait()
    own = jnp.maximum(pairs[6, 0] - OWN_DONE, 0)
    side = jnp.maximum(pairs[7, 0] - SIDE_DONE, 0)

    def measure(row, source, task):
        lane = jnp.minimum(task, 127)
        return squares(source[pairs[row + 1, lane]], target[pairs[row, lane]])

    def add(row, vec, task, square):
        lanes = pl.ds(pl.multiple_of(pairs[row, task] * POINTS, POINTS), POINTS)
        weight = pairs[row + 2, task].astype(F32) * SCALE
        out[:, lanes] += weight * dot(vec[pairs[row + 1, task]], tile_of(square))

    def single(n, carry):
        add(0, own_vec, OWN_DONE + n, measure(0, own_source, OWN_DONE + n))
        return carry

    lax.fori_loop(0, own, single, 0)

    dist[0] = measure(3, side_source, SIDE_DONE)

    def turns(width, first):
        def turn(n, carry):
            for k in range(width):
                task = first + n * width + k
                square = dist[k % 2]
                dist[1 - k % 2] = measure(3, side_source, task + 1)
                add(3, side_vec, task, square)
            return carry

        return turn

    whole = side // TURN
    rest = side % TURN
    lax.fori_loop(0, whole, turns(TURN, SIDE_DONE), 0)
    lax.fori_loop(0, rest // 2, turns(2, SIDE_DONE + whole * TURN), 0)
    lax.fori_loop(0, rest % 2, turns(1, SIDE_DONE + side - 1), 0)


def near_field(total, pairs, *arrays):
    return pl.pallas_call(
        near_kernel,
        out_shape=jax.ShapeDtypeStruct((PROBES, WIDTH), F32),
        in_specs=[ANY] + [VMEM] * 6,
        out_specs=VMEM,
        scratch_shapes=[
            pltpu.SMEM((8, 128), I32),
            pltpu.VMEM((2, POINTS, POINTS), F32),
            pltpu.SemaphoreType.DMA((1,)),
        ],
        compiler_params=pltpu.CompilerParams(vmem_limit_bytes=VMEM_LIMIT),
    )(pairs, total, *arrays)


def local(gy_count, coords, vectors, *rest):
    matrices, near_list, near_count = rest[:-2], rest[-2], rest[-1]
    arrays = (coords, vectors, near_list, near_count, *matrices)
    return near_field(*far_field(gy_count, *(pltpu.with_memory_space_constraint(a, pltpu.HBM) for a in arrays)))


def solution(mesh):
    both = ("gx", "gy")
    return jax.shard_map(
        functools.partial(local, mesh.shape["gy"]),
        mesh=mesh,
        in_specs=(
            P(None, both),
            P(None, both),
            P(both, None, None),
            P(both, None, None),
            P(both, None, None),
            P("gx", None, None),
            P(both, None, None, None),
            P("gx", None, None, None),
            P("gx", None, None, None),
            P(both, None),
            P("gx", None),
            P("gx", None),
            P(both, None),
            P(both),
        ),
        out_specs=P(None, both),
        check_vma=False,
    )
```

```python
import functools
import math

import jax
import jax.numpy as jnp
from jax import lax
from jax.experimental import pallas as pl
from jax.experimental.pallas import tpu as pltpu
from jax.sharding import PartitionSpec as P

MESH = pl.DeviceIdType.MESH
F32 = jnp.float32
BF = jnp.bfloat16
I32 = jnp.int32
BOXES = 8
POINTS = 512
PROBES = 16
RANK = 128
NEAR = 16
FAR = 6
WIDTH = BOXES * POINTS
GX = 8
LINE = 16
LINES = 4
GROUP = 8
TURN = 6
OWN_TURNS = 5
MID_TURNS = 1
LAST_TURNS = 3
OWN_DONE = OWN_TURNS * TURN
SIDE_DONE = (MID_TURNS + LAST_TURNS) * TURN
SCALE = POINTS**-0.5
VMEM_LIMIT = 30 << 20
HBM = pl.BlockSpec(memory_space=pltpu.HBM)
ANY = pl.BlockSpec(memory_space=pl.ANY)
VMEM = pl.BlockSpec(memory_space=pltpu.VMEM)
SMEM = pl.BlockSpec(memory_space=pltpu.SMEM)


def dot(a, b):
    return jnp.dot(a, b, preferred_element_type=F32)


def dot_t(a, b):
    return lax.dot_general(a, b, (((1,), (1,)), ((), ())), preferred_element_type=F32)


def span(box):
    return slice(box * POINTS, (box + 1) * POINTS)


def gather(ref, index_of):
    return jnp.concatenate([ref[index_of(f)] for f in range(FAR)], axis=1)


def squares(source, target):
    return lax.dot_general(source, target, (((0,), (0,)), ((), ())), preferred_element_type=F32)


def tile_of(square):
    square = jnp.maximum(square, 1e-30)
    return jnp.exp2((square * -math.log2(math.e)) * lax.rsqrt(square)).astype(BF)


def norm_parts(parts):
    norm = parts[0] * parts[0] + parts[1] * parts[1] + parts[2] * parts[2]
    high = norm.astype(BF).astype(F32)
    rest = norm - high
    middle = rest.astype(BF).astype(F32)
    return [high, middle, rest - middle]


def set_rows(raw, first, values):
    for n, value in enumerate(values):
        for box in range(BOXES):
            raw[box, first + n : first + n + 1, :] = value[box : box + 1, :]


def compact(times, box, place):
    count = times.shape[0]
    across = lax.broadcasted_iota(I32, (count, 128), 1)
    down = lax.broadcasted_iota(I32, (count, 128), 0)
    live = jnp.broadcast_to(jnp.where(times > 0, 1, 0), (count, 128))
    along = jnp.sum(jnp.where(across == down, live, 0), axis=0, keepdims=True)
    rank = jnp.sum(jnp.where(across < down, along, 0), axis=1, keepdims=True)
    hit = (rank == across) & (live > 0)
    rows = [jnp.sum(jnp.where(hit, value, 0), axis=0, keepdims=True) for value in (box, place, times)]
    return rows, jnp.sum(live, axis=0, keepdims=True)


def pair_lists(near_list, near_count, gy, gy_count, out):
    place = lax.broadcasted_iota(I32, (3 * BOXES, NEAR), 0)
    slot = lax.broadcasted_iota(I32, (3 * BOXES, NEAR), 1)
    column = gy + place // BOXES - 1
    inside = (column >= 0) & (column < gy_count)
    own, side = [], []
    for box in range(BOXES):
        named = (near_list[box : box + 1, :] == place) & (slot < near_count[box]) & inside
        times = jnp.sum(jnp.where(named, 1, 0), axis=1, keepdims=True)
        own.append(times[BOXES : 2 * BOXES])
        side += [times[:BOXES], times[2 * BOXES :]]
    own, side = jnp.concatenate(own, axis=0), jnp.concatenate(side, axis=0)
    n = lax.broadcasted_iota(I32, own.shape, 0)
    own_rows, own_count = compact(own, n // BOXES, n % BOXES)
    n = lax.broadcasted_iota(I32, side.shape, 0)
    side_rows, side_count = compact(side, n // (2 * BOXES), n % (2 * BOXES))
    for n, row in enumerate(own_rows + side_rows + [own_count, side_count]):
        out[n : n + 1, :] = row


def far_kernel(
    gy_count,
    coords_hbm,
    vectors_hbm,
    list_hbm,
    count_hbm,
    basis_hbm,
    leaf_hbm,
    mid_hbm,
    top_hbm,
    one_hbm,
    two_hbm,
    three_hbm,
    far_one_hbm,
    far_two_hbm,
    far_three_hbm,
    total,
    pairs,
    own_vec_out,
    side_vec_out,
    own_source_out,
    side_source_out,
    target_out,
    own_vec,
    side_vec,
    own_source,
    side_source,
    target,
    coords,
    vectors,
    near_list,
    near_count,
    basis,
    leaf_up,
    mid_up,
    top_up,
    couple_one,
    couple_two,
    couple_three,
    far_one,
    far_two,
    far_three,
    pos_f32,
    pos,
    side_pos,
    raw,
    dist,
    tasks,
    down_three,
    down_leaf,
    toward,
    level_two,
    level_three,
    row_one,
    load_sem,
    task_sem,
    out_sem,
    side_send,
    side_recv,
    toward_sem,
    line_sem,
    two_sem,
    row_sem,
    three_sem,
):
    gx = lax.axis_index("gx")
    gy = lax.axis_index("gy")
    x = gy // LINE
    z = gy % LINE
    group = gy // GROUP
    loads = [
        pltpu.make_async_copy(source, goal, load_sem.at[n])
        for n, (source, goal) in enumerate(
            (
                (vectors_hbm, vectors),
                (coords_hbm, coords),
                (list_hbm, near_list),
                (count_hbm, near_count),
                (basis_hbm, basis),
                (leaf_hbm, leaf_up),
                (mid_hbm, mid_up),
                (top_hbm, top_up),
                (two_hbm.at[group], couple_two),
                (three_hbm, couple_three),
                (one_hbm, couple_one),
                (far_one_hbm, far_one),
                (far_two_hbm, far_two),
                (far_three_hbm, far_three),
            )
        )
    ]
    for n in (0, 1, 4, 5, 6):
        loads[n].start()

    right = (gy + 1) % gy_count
    left = (gy + gy_count - 1) % gy_count

    def in_line(step):
        return x * LINE + (z + step) % LINE

    def in_plane(step):
        return ((x + step) % LINES) * LINE + z

    barrier = pltpu.get_barrier_semaphore()

    def greet(peer):
        pl.semaphore_signal(barrier, inc=1, device_id=peer, device_id_type=MESH)

    def greet_line(n, carry):
        greet((gx, in_line(n)))
        return carry

    def greet_three(n, carry):
        greet(((gx + n) % GX, gy))
        return carry

    lax.fori_loop(1, LINE, greet_line, 0)
    for n in range(1, LINES):
        greet((gx, in_plane(n)))
    lax.fori_loop(1, GX, greet_three, 0)
    greet((gx, left))
    greet((gx, right))
    for n in (2, 3, *range(7, 14)):
        loads[n].start()

    loads[1].wait()
    for comp in range(3):
        for box in range(BOXES):
            row = comp * BOXES + box
            pos_f32[row : row + 1, :] = coords[comp : comp + 1, span(box)].astype(F32)
    pos_f32[24:32, :] = jnp.zeros((8, POINTS), F32)
    pos[...] = pos_f32[...].astype(BF)

    loads[0].wait()
    for box in range(BOXES):
        own_vec[box] = vectors[:, span(box)].astype(BF)
    loads[4].wait()
    loads[5].wait()
    leaf = jnp.concatenate([dot(own_vec[b], basis[b]).astype(BF) for b in range(BOXES)], axis=1)
    ups = leaf_up[...].reshape(BOXES * RANK, RANK)
    one = dot(leaf, ups).astype(BF)
    row_one[gy] = one
    loads[6].wait()
    toward[z] = dot(one, mid_up[0]).astype(BF)

    def copy(ref, sems, peer):
        return pltpu.make_async_remote_copy(
            src_ref=ref,
            dst_ref=ref,
            send_sem=sems.at[0],
            recv_sem=sems.at[1],
            device_id=peer,
            device_id_type=MESH,
        )

    def start_far_first(ref, sems):
        for n in (8, 7, 9, 6, 10, 5, 11, 4, 12, 3, 13, 2, 14, 1, 15):
            copy(ref, sems, (gx, in_line(n))).start()

    def start_plane(ref, sems):
        for n in (2, 1, 3):
            copy(ref, sems, (gx, in_plane(n))).start()

    def start_three(ref, sems):
        for n in (4, 5, 3, 2, 6, 7, 1):
            copy(ref, sems, ((gx + n) % GX, gy)).start()

    line_peer, plane_peer, three_peer = (gx, in_line(1)), (gx, in_plane(1)), ((gx + 1) % GX, gy)
    all_toward = copy(toward.at[pl.ds(0, LINE - 1)], toward_sem, line_peer)
    all_lines = copy(row_one.at[pl.ds(0, LINE - 1)], line_sem, line_peer)
    all_two = copy(level_two.at[pl.ds(0, LINES - 1)], two_sem, plane_peer)
    all_rows = copy(row_one.at[pl.ds(0, (LINES - 1) * LINE)], row_sem, plane_peer)
    all_three = copy(level_three.at[pl.ds(0, GX - 1)], three_sem, three_peer)

    sides = []
    for n, (source, goal, rows) in enumerate(((own_vec, side_vec, 8), (pos, side_pos, 32))):
        for side, peer in ((0, right), (1, left)):
            sides.append(
                pltpu.make_async_remote_copy(
                    src_ref=source,
                    dst_ref=goal.at[pl.ds(side * rows, rows)],
                    send_sem=side_send.at[2 * n + side],
                    recv_sem=side_recv.at[2 * n + side],
                    device_id=(gx, peer),
                    device_id_type=MESH,
                )
            )

    def enter(rows_first):
        pl.semaphore_wait(barrier, LINE - 1 + LINES - 1 + GX - 1 + 2)
        start_far_first(toward.at[z], toward_sem)
        if rows_first:
            start_far_first(row_one.at[gy], line_sem)
        for side_copy in sides:
            side_copy.start()
        if not rows_first:
            start_far_first(row_one.at[gy], line_sem)

    late = (z // 8) * (1 - z // 12)
    ahead = (1 - z // 8) * (OWN_TURNS - (z // 4) * (z // 2 - 1)) + z // 12

    pl.when(late == 1)(functools.partial(enter, True))

    raw[...] = jnp.zeros_like(raw)
    ones = [jnp.ones((BOXES, POINTS), F32)] * 3
    parts = [pos_f32[n * BOXES : (n + 1) * BOXES, :] for n in range(3)]
    norms = norm_parts(parts)
    set_rows(raw, 0, parts + ones + norms)
    target[...] = raw[...].astype(BF)
    set_rows(raw, 0, [-2.0 * part for part in parts] + norms + ones)
    own_source[...] = raw[...].astype(BF)
    outs = [
        pltpu.make_async_copy(source, goal, out_sem.at[n])
        for n, (source, goal) in enumerate(
            (
                (own_vec, own_vec_out),
                (own_source, own_source_out),
                (target, target_out),
                (side_vec, side_vec_out),
                (side_source, side_source_out),
            )
        )
    ]
    for out_copy in outs[:3]:
        out_copy.start()
    total[...] = jnp.zeros_like(total)
    loads[2].wait()
    loads[3].wait()
    pair_lists(near_list, near_count, gy, gy_count, pairs)
    task_copy = pltpu.make_async_copy(pairs, tasks, task_sem.at[0])
    task_copy.start()

    task_copy.wait()

    def begin(first_row, source_ref, task):
        dist[0] = squares(source_ref[tasks[first_row + 1, task]], target[tasks[first_row, task]])

    def fill(first_row, source_ref, vec_ref, first, last):
        def turn(n, carry):
            for k in range(TURN):
                task = n * TURN + k
                square = dist[k % 2]
                dist[1 - k % 2] = squares(
                    source_ref[tasks[first_row + 1, task + 1]], target[tasks[first_row, task + 1]]
                )
                part = dot(vec_ref[tasks[first_row + 1, task]], tile_of(square))
                box = tasks[first_row, task]
                weight = tasks[first_row + 2, task].astype(F32) * SCALE
                for b in range(BOXES):
                    total[:, span(b)] += jnp.where(box == b, weight, 0.0) * part
            return carry

        lax.fori_loop(first, last, turn, 0)

    begin(0, own_source, 0)
    fill(0, own_source, own_vec, 0, ahead)

    pl.when(late == 0)(functools.partial(enter, False))

    fill(0, own_source, own_vec, ahead, OWN_TURNS)

    for load in loads[7:]:
        load.wait()
    down = dot(mid_up[0], top_up[group]).astype(BF)
    down_three[...] = dot_t(couple_three[0].reshape(FAR * RANK, RANK), down).astype(BF)
    for b in range(BOXES):
        down_leaf[b * POINTS : (b + 1) * POINTS, :] = dot(basis[b], leaf_up[b]).astype(BF)

    all_toward.wait_recv()
    for half in range(2):
        two = jnp.zeros((PROBES, RANK), F32)
        for n in range(GROUP):
            two = two + toward[half * GROUP + n].astype(F32)
        level_two[x, half] = two.astype(BF)
    start_plane(level_two.at[x], two_sem)
    for side_copy in sides:
        side_copy.wait_recv()
    for side in range(2):
        first = side * 32
        near = side_pos[first : first + 24, :].astype(F32)
        parts = [near[n * BOXES : (n + 1) * BOXES, :] for n in range(3)]
        set_rows(raw, 0, [-2.0 * part for part in parts] + norm_parts(parts))
        side_source[side * BOXES : (side + 1) * BOXES] = raw[...].astype(BF)
    for out_copy in outs[3:]:
        out_copy.start()
    begin(3, side_source, 0)
    fill(3, side_source, side_vec, 0, MID_TURNS)

    all_two.wait_recv()
    twos = jnp.concatenate([level_two[n // 2, n % 2] for n in range(8)], axis=1)
    level_three[gx] = dot(twos, top_up[...].reshape(8 * RANK, RANK)).astype(BF)
    start_three(level_three.at[gx], three_sem)
    all_lines.wait_recv()
    start_plane(row_one.at[pl.ds(x * LINE, LINE)], row_sem)

    source_two = gather(level_two, lambda f: (far_two[group, f] // 2, far_two[group, f] % 2))
    local_two = dot(source_two, couple_two[...].reshape(FAR * RANK, RANK))
    local_one = dot_t(local_two.astype(BF), mid_up[0])
    fill(3, side_source, side_vec, MID_TURNS, MID_TURNS + LAST_TURNS)

    all_three.wait_recv()
    local_one = local_one + dot(gather(level_three, lambda f: far_three[0, f]), down_three[...])
    all_rows.wait_recv()
    local_one = local_one + dot(
        gather(row_one, lambda f: far_one[0, f]), couple_one[0].reshape(FAR * RANK, RANK)
    )
    total[...] += dot_t(local_one.astype(BF), down_leaf[...])

    for out_copy in outs:
        out_copy.wait()
    for side_copy in sides:
        side_copy.wait_send()
    for exchange in (all_toward, all_lines, all_two, all_rows, all_three):
        exchange.wait_send()


def far_field(gy_count, *arrays):
    dma = pltpu.SemaphoreType.DMA
    boxes = (BOXES, PROBES, POINTS)
    sides = (2 * BOXES, PROBES, POINTS)
    return pl.pallas_call(
        functools.partial(far_kernel, gy_count),
        out_shape=(
            jax.ShapeDtypeStruct((PROBES, WIDTH), F32),
            jax.ShapeDtypeStruct((8, 128), I32),
            jax.ShapeDtypeStruct(boxes, BF),
            jax.ShapeDtypeStruct(sides, BF),
            jax.ShapeDtypeStruct(boxes, BF),
            jax.ShapeDtypeStruct(sides, BF),
            jax.ShapeDtypeStruct(boxes, BF),
        ),
        in_specs=[HBM] * 14,
        out_specs=(VMEM, VMEM) + (ANY,) * 5,
        scratch_shapes=[
            pltpu.VMEM(boxes, BF),
            pltpu.VMEM(sides, BF),
            pltpu.VMEM(boxes, BF),
            pltpu.VMEM(sides, BF),
            pltpu.VMEM(boxes, BF),
            pltpu.VMEM((3, WIDTH), BF),
            pltpu.VMEM((PROBES, WIDTH), F32),
            pltpu.VMEM((BOXES, NEAR), I32),
            pltpu.SMEM((BOXES,), I32),
            pltpu.VMEM((BOXES, POINTS, RANK), BF),
            pltpu.VMEM((BOXES, RANK, RANK), BF),
            pltpu.VMEM((1, RANK, RANK), BF),
            pltpu.VMEM((8, RANK, RANK), BF),
            pltpu.VMEM((1, FAR, RANK, RANK), BF),
            pltpu.VMEM((FAR, RANK, RANK), BF),
            pltpu.VMEM((1, FAR, RANK, RANK), BF),
            pltpu.SMEM((1, FAR), I32),
            pltpu.SMEM((8, FAR), I32),
            pltpu.SMEM((1, FAR), I32),
            pltpu.VMEM((32, POINTS), F32),
            pltpu.VMEM((32, POINTS), BF),
            pltpu.VMEM((64, POINTS), BF),
            pltpu.VMEM(boxes, F32),
            pltpu.VMEM((2, POINTS, POINTS), F32),
            pltpu.SMEM((8, 128), I32),
            pltpu.VMEM((FAR * RANK, RANK), BF),
            pltpu.VMEM((WIDTH, RANK), BF),
            pltpu.VMEM((LINE, PROBES, RANK), BF),
            pltpu.VMEM((LINES, 2, PROBES, RANK), BF),
            pltpu.VMEM((GX, PROBES, RANK), BF),
            pltpu.VMEM((LINE * LINES, PROBES, RANK), BF),
            dma((14,)),
            dma((1,)),
            dma((5,)),
            dma((4,)),
            dma((4,)),
            dma((2,)),
            dma((2,)),
            dma((2,)),
            dma((2,)),
            dma((2,)),
        ],
        compiler_params=pltpu.CompilerParams(
            collective_id=0, has_side_effects=True, vmem_limit_bytes=VMEM_LIMIT
        ),
    )(*arrays)


def near_kernel(pairs_hbm, total, own_vec, side_vec, own_source, side_source, target, out, pairs, dist, sem):
    load = pltpu.make_async_copy(pairs_hbm, pairs, sem.at[0])
    load.start()
    out[...] = total[...]
    load.wait()
    own = jnp.maximum(pairs[6, 0] - OWN_DONE, 0)
    side = jnp.maximum(pairs[7, 0] - SIDE_DONE, 0)

    def measure(row, source, task):
        lane = jnp.minimum(task, 127)
        return squares(source[pairs[row + 1, lane]], target[pairs[row, lane]])

    def add(row, vec, task, square):
        lanes = pl.ds(pl.multiple_of(pairs[row, task] * POINTS, POINTS), POINTS)
        weight = pairs[row + 2, task].astype(F32) * SCALE
        out[:, lanes] += weight * dot(vec[pairs[row + 1, task]], tile_of(square))

    def single(n, carry):
        add(0, own_vec, OWN_DONE + n, measure(0, own_source, OWN_DONE + n))
        return carry

    lax.fori_loop(0, own, single, 0)

    dist[0] = measure(3, side_source, SIDE_DONE)

    def turns(width, first):
        def turn(n, carry):
            for k in range(width):
                task = first + n * width + k
                square = dist[k % 2]
                dist[1 - k % 2] = measure(3, side_source, task + 1)
                add(3, side_vec, task, square)
            return carry

        return turn

    whole = side // TURN
    rest = side % TURN
    lax.fori_loop(0, whole, turns(TURN, SIDE_DONE), 0)
    lax.fori_loop(0, rest // 2, turns(2, SIDE_DONE + whole * TURN), 0)
    lax.fori_loop(0, rest % 2, turns(1, SIDE_DONE + side - 1), 0)


def near_field(total, pairs, *arrays):
    return pl.pallas_call(
        near_kernel,
        out_shape=jax.ShapeDtypeStruct((PROBES, WIDTH), F32),
        in_specs=[ANY] + [VMEM] * 6,
        out_specs=VMEM,
        scratch_shapes=[
            pltpu.SMEM((8, 128), I32),
            pltpu.VMEM((2, POINTS, POINTS), F32),
            pltpu.SemaphoreType.DMA((1,)),
        ],
        compiler_params=pltpu.CompilerParams(vmem_limit_bytes=VMEM_LIMIT),
    )(pairs, total, *arrays)


def local(gy_count, coords, vectors, *rest):
    matrices, near_list, near_count = rest[:-2], rest[-2], rest[-1]
    arrays = (coords, vectors, near_list, near_count, *matrices)
    return near_field(*far_field(gy_count, *(pltpu.with_memory_space_constraint(a, pltpu.HBM) for a in arrays)))


def solution(mesh):
    both = ("gx", "gy")
    return jax.shard_map(
        functools.partial(local, mesh.shape["gy"]),
        mesh=mesh,
        in_specs=(
            P(None, both),
            P(None, both),
            P(both, None, None),
            P(both, None, None),
            P(both, None, None),
            P("gx", None, None),
            P(both, None, None, None),
            P("gx", None, None, None),
            P("gx", None, None, None),
            P(both, None),
            P("gx", None),
            P("gx", None),
            P(both, None),
            P(both),
        ),
        out_specs=P(None, both),
        check_vma=False,
    )
```

```python
import functools
import math

import jax
import jax.numpy as jnp
from jax import lax
from jax.experimental import pallas as pl
from jax.experimental.pallas import tpu as pltpu
from jax.sharding import PartitionSpec as P

MESH = pl.DeviceIdType.MESH
F32 = jnp.float32
BF = jnp.bfloat16
I32 = jnp.int32
BOXES = 8
POINTS = 512
PROBES = 16
RANK = 128
NEAR = 16
FAR = 6
WIDTH = BOXES * POINTS
GX = 8
LINE = 16
LINES = 4
GROUP = 8
TURN = 6
OWN_TURNS = 5
MID_TURNS = 1
LAST_TURNS = 3
OWN_DONE = OWN_TURNS * TURN
SIDE_DONE = (MID_TURNS + LAST_TURNS) * TURN
SCALE = POINTS**-0.5
VMEM_LIMIT = 30 << 20
HBM = pl.BlockSpec(memory_space=pltpu.HBM)
ANY = pl.BlockSpec(memory_space=pl.ANY)
VMEM = pl.BlockSpec(memory_space=pltpu.VMEM)
SMEM = pl.BlockSpec(memory_space=pltpu.SMEM)


def dot(a, b):
    return jnp.dot(a, b, preferred_element_type=F32)


def dot_t(a, b):
    return lax.dot_general(a, b, (((1,), (1,)), ((), ())), preferred_element_type=F32)


def span(box):
    return slice(box * POINTS, (box + 1) * POINTS)


def gather(ref, index_of):
    return jnp.concatenate([ref[index_of(f)] for f in range(FAR)], axis=1)


def squares(source, target):
    return lax.dot_general(source, target, (((0,), (0,)), ((), ())), preferred_element_type=F32)


def tile_of(square):
    square = jnp.maximum(square, 1e-30)
    return jnp.exp2((square * -math.log2(math.e)) * lax.rsqrt(square)).astype(BF)


def norm_parts(parts):
    norm = parts[0] * parts[0] + parts[1] * parts[1] + parts[2] * parts[2]
    high = norm.astype(BF).astype(F32)
    rest = norm - high
    middle = rest.astype(BF).astype(F32)
    return [high, middle, rest - middle]


def set_rows(raw, first, values):
    for n, value in enumerate(values):
        for box in range(BOXES):
            raw[box, first + n : first + n + 1, :] = value[box : box + 1, :]


def compact(times, box, place):
    count = times.shape[0]
    across = lax.broadcasted_iota(I32, (count, 128), 1)
    down = lax.broadcasted_iota(I32, (count, 128), 0)
    live = jnp.broadcast_to(jnp.where(times > 0, 1, 0), (count, 128))
    along = jnp.sum(jnp.where(across == down, live, 0), axis=0, keepdims=True)
    rank = jnp.sum(jnp.where(across < down, along, 0), axis=1, keepdims=True)
    hit = (rank == across) & (live > 0)
    rows = [jnp.sum(jnp.where(hit, value, 0), axis=0, keepdims=True) for value in (box, place, times)]
    return rows, jnp.sum(live, axis=0, keepdims=True)


def pair_lists(near_list, near_count, gy, gy_count, out):
    place = lax.broadcasted_iota(I32, (3 * BOXES, NEAR), 0)
    slot = lax.broadcasted_iota(I32, (3 * BOXES, NEAR), 1)
    column = gy + place // BOXES - 1
    inside = (column >= 0) & (column < gy_count)
    own, side = [], []
    for box in range(BOXES):
        named = (near_list[box : box + 1, :] == place) & (slot < near_count[box]) & inside
        times = jnp.sum(jnp.where(named, 1, 0), axis=1, keepdims=True)
        own.append(times[BOXES : 2 * BOXES])
        side += [times[:BOXES], times[2 * BOXES :]]
    own, side = jnp.concatenate(own, axis=0), jnp.concatenate(side, axis=0)
    n = lax.broadcasted_iota(I32, own.shape, 0)
    own_rows, own_count = compact(own, n // BOXES, n % BOXES)
    n = lax.broadcasted_iota(I32, side.shape, 0)
    side_rows, side_count = compact(side, n // (2 * BOXES), n % (2 * BOXES))
    for n, row in enumerate(own_rows + side_rows + [own_count, side_count]):
        out[n : n + 1, :] = row


def far_kernel(
    gy_count,
    coords_hbm,
    vectors_hbm,
    list_hbm,
    count_hbm,
    basis_hbm,
    leaf_hbm,
    mid_hbm,
    top_hbm,
    one_hbm,
    two_hbm,
    three_hbm,
    far_one_hbm,
    far_two_hbm,
    far_three_hbm,
    total,
    pairs,
    own_vec,
    side_vec,
    own_source,
    side_source,
    target,
    coords,
    vectors,
    near_list,
    near_count,
    basis,
    leaf_up,
    mid_up,
    top_up,
    couple_one,
    couple_two,
    couple_three,
    far_one,
    far_two,
    far_three,
    pos_f32,
    pos,
    side_pos,
    raw,
    dist,
    tasks,
    down_three,
    down_leaf,
    toward,
    level_two,
    level_three,
    row_one,
    load_sem,
    task_sem,
    side_send,
    side_recv,
    toward_sem,
    line_sem,
    two_sem,
    row_sem,
    three_sem,
):
    gx = lax.axis_index("gx")
    gy = lax.axis_index("gy")
    x = gy // LINE
    z = gy % LINE
    group = gy // GROUP
    loads = [
        pltpu.make_async_copy(source, goal, load_sem.at[n])
        for n, (source, goal) in enumerate(
            (
                (vectors_hbm, vectors),
                (coords_hbm, coords),
                (list_hbm, near_list),
                (count_hbm, near_count),
                (basis_hbm, basis),
                (leaf_hbm, leaf_up),
                (mid_hbm, mid_up),
                (top_hbm, top_up),
                (two_hbm.at[group], couple_two),
                (three_hbm, couple_three),
                (one_hbm, couple_one),
                (far_one_hbm, far_one),
                (far_two_hbm, far_two),
                (far_three_hbm, far_three),
            )
        )
    ]
    for n in (0, 1, 4, 5, 6):
        loads[n].start()

    right = (gy + 1) % gy_count
    left = (gy + gy_count - 1) % gy_count

    def in_line(step):
        return x * LINE + (z + step) % LINE

    def in_plane(step):
        return ((x + step) % LINES) * LINE + z

    barrier = pltpu.get_barrier_semaphore()

    def greet(peer):
        pl.semaphore_signal(barrier, inc=1, device_id=peer, device_id_type=MESH)

    def greet_line(n, carry):
        greet((gx, in_line(n)))
        return carry

    def greet_three(n, carry):
        greet(((gx + n) % GX, gy))
        return carry

    lax.fori_loop(1, LINE, greet_line, 0)
    for n in range(1, LINES):
        greet((gx, in_plane(n)))
    lax.fori_loop(1, GX, greet_three, 0)
    greet((gx, left))
    greet((gx, right))
    for n in (2, 3, *range(7, 14)):
        loads[n].start()

    loads[1].wait()
    for comp in range(3):
        for box in range(BOXES):
            row = comp * BOXES + box
            pos_f32[row : row + 1, :] = coords[comp : comp + 1, span(box)].astype(F32)
    pos_f32[24:32, :] = jnp.zeros((8, POINTS), F32)
    pos[...] = pos_f32[...].astype(BF)

    loads[0].wait()
    for box in range(BOXES):
        own_vec[box] = vectors[:, span(box)].astype(BF)
    loads[4].wait()
    loads[5].wait()
    leaf = jnp.concatenate([dot(own_vec[b], basis[b]).astype(BF) for b in range(BOXES)], axis=1)
    ups = leaf_up[...].reshape(BOXES * RANK, RANK)
    one = dot(leaf, ups).astype(BF)
    row_one[gy] = one
    loads[6].wait()
    toward[z] = dot(one, mid_up[0]).astype(BF)

    def copy(ref, sems, peer):
        return pltpu.make_async_remote_copy(
            src_ref=ref,
            dst_ref=ref,
            send_sem=sems.at[0],
            recv_sem=sems.at[1],
            device_id=peer,
            device_id_type=MESH,
        )

    def start_far_first(ref, sems):
        for n in (8, 7, 9, 6, 10, 5, 11, 4, 12, 3, 13, 2, 14, 1, 15):
            copy(ref, sems, (gx, in_line(n))).start()

    def start_plane(ref, sems):
        for n in (2, 1, 3):
            copy(ref, sems, (gx, in_plane(n))).start()

    def start_three(ref, sems):
        for n in (4, 5, 3, 2, 6, 7, 1):
            copy(ref, sems, ((gx + n) % GX, gy)).start()

    line_peer, plane_peer, three_peer = (gx, in_line(1)), (gx, in_plane(1)), ((gx + 1) % GX, gy)
    all_toward = copy(toward.at[pl.ds(0, LINE - 1)], toward_sem, line_peer)
    all_lines = copy(row_one.at[pl.ds(0, LINE - 1)], line_sem, line_peer)
    all_two = copy(level_two.at[pl.ds(0, LINES - 1)], two_sem, plane_peer)
    all_rows = copy(row_one.at[pl.ds(0, (LINES - 1) * LINE)], row_sem, plane_peer)
    all_three = copy(level_three.at[pl.ds(0, GX - 1)], three_sem, three_peer)

    sides = []
    for n, (source, goal, rows) in enumerate(((own_vec, side_vec, 8), (pos, side_pos, 32))):
        for side, peer in ((0, right), (1, left)):
            sides.append(
                pltpu.make_async_remote_copy(
                    src_ref=source,
                    dst_ref=goal.at[pl.ds(side * rows, rows)],
                    send_sem=side_send.at[2 * n + side],
                    recv_sem=side_recv.at[2 * n + side],
                    device_id=(gx, peer),
                    device_id_type=MESH,
                )
            )

    def enter(rows_first):
        pl.semaphore_wait(barrier, LINE - 1 + LINES - 1 + GX - 1 + 2)
        start_far_first(toward.at[z], toward_sem)
        if rows_first:
            start_far_first(row_one.at[gy], line_sem)
        for side_copy in sides:
            side_copy.start()
        if not rows_first:
            start_far_first(row_one.at[gy], line_sem)

    late = (z // 8) * (1 - z // 12)
    ahead = (1 - z // 8) * (OWN_TURNS - (z // 4) * (z // 2 - 1)) + z // 12

    pl.when(late == 1)(functools.partial(enter, True))

    raw[...] = jnp.zeros_like(raw)
    ones = [jnp.ones((BOXES, POINTS), F32)] * 3
    parts = [pos_f32[n * BOXES : (n + 1) * BOXES, :] for n in range(3)]
    norms = norm_parts(parts)
    set_rows(raw, 0, parts + ones + norms)
    target[...] = raw[...].astype(BF)
    set_rows(raw, 0, [-2.0 * part for part in parts] + norms + ones)
    own_source[...] = raw[...].astype(BF)
    total[...] = jnp.zeros_like(total)
    loads[2].wait()
    loads[3].wait()
    pair_lists(near_list, near_count, gy, gy_count, pairs)
    task_copy = pltpu.make_async_copy(pairs, tasks, task_sem.at[0])
    task_copy.start()

    task_copy.wait()

    def begin(first_row, source_ref, task):
        dist[0] = squares(source_ref[tasks[first_row + 1, task]], target[tasks[first_row, task]])

    def fill(first_row, source_ref, vec_ref, first, last):
        def turn(n, carry):
            for k in range(TURN):
                task = n * TURN + k
                square = dist[k % 2]
                dist[1 - k % 2] = squares(
                    source_ref[tasks[first_row + 1, task + 1]], target[tasks[first_row, task + 1]]
                )
                part = dot(vec_ref[tasks[first_row + 1, task]], tile_of(square))
                box = tasks[first_row, task]
                weight = tasks[first_row + 2, task].astype(F32) * SCALE
                for b in range(BOXES):
                    total[:, span(b)] += jnp.where(box == b, weight, 0.0) * part
            return carry

        lax.fori_loop(first, last, turn, 0)

    begin(0, own_source, 0)
    fill(0, own_source, own_vec, 0, ahead)

    pl.when(late == 0)(functools.partial(enter, False))

    fill(0, own_source, own_vec, ahead, OWN_TURNS)

    for load in loads[7:]:
        load.wait()
    down = dot(mid_up[0], top_up[group]).astype(BF)
    down_three[...] = dot_t(couple_three[0].reshape(FAR * RANK, RANK), down).astype(BF)
    for b in range(BOXES):
        down_leaf[b * POINTS : (b + 1) * POINTS, :] = dot(basis[b], leaf_up[b]).astype(BF)

    all_toward.wait_recv()
    for half in range(2):
        two = jnp.zeros((PROBES, RANK), F32)
        for n in range(GROUP):
            two = two + toward[half * GROUP + n].astype(F32)
        level_two[x, half] = two.astype(BF)
    start_plane(level_two.at[x], two_sem)
    for side_copy in sides:
        side_copy.wait_recv()
    for side in range(2):
        first = side * 32
        near = side_pos[first : first + 24, :].astype(F32)
        parts = [near[n * BOXES : (n + 1) * BOXES, :] for n in range(3)]
        set_rows(raw, 0, [-2.0 * part for part in parts] + norm_parts(parts))
        side_source[side * BOXES : (side + 1) * BOXES] = raw[...].astype(BF)
    begin(3, side_source, 0)
    fill(3, side_source, side_vec, 0, MID_TURNS)

    all_two.wait_recv()
    twos = jnp.concatenate([level_two[n // 2, n % 2] for n in range(8)], axis=1)
    level_three[gx] = dot(twos, top_up[...].reshape(8 * RANK, RANK)).astype(BF)
    start_three(level_three.at[gx], three_sem)
    all_lines.wait_recv()
    start_plane(row_one.at[pl.ds(x * LINE, LINE)], row_sem)

    source_two = gather(level_two, lambda f: (far_two[group, f] // 2, far_two[group, f] % 2))
    local_two = dot(source_two, couple_two[...].reshape(FAR * RANK, RANK))
    local_one = dot_t(local_two.astype(BF), mid_up[0])
    fill(3, side_source, side_vec, MID_TURNS, MID_TURNS + LAST_TURNS)

    all_three.wait_recv()
    local_one = local_one + dot(gather(level_three, lambda f: far_three[0, f]), down_three[...])
    all_rows.wait_recv()
    local_one = local_one + dot(
        gather(row_one, lambda f: far_one[0, f]), couple_one[0].reshape(FAR * RANK, RANK)
    )
    total[...] += dot_t(local_one.astype(BF), down_leaf[...])

    for side_copy in sides:
        side_copy.wait_send()
    for exchange in (all_toward, all_lines, all_two, all_rows, all_three):
        exchange.wait_send()


def far_field(gy_count, *arrays):
    dma = pltpu.SemaphoreType.DMA
    boxes = (BOXES, PROBES, POINTS)
    sides = (2 * BOXES, PROBES, POINTS)
    return pl.pallas_call(
        functools.partial(far_kernel, gy_count),
        out_shape=(
            jax.ShapeDtypeStruct((PROBES, WIDTH), F32),
            jax.ShapeDtypeStruct((8, 128), I32),
            jax.ShapeDtypeStruct(boxes, BF),
            jax.ShapeDtypeStruct(sides, BF),
            jax.ShapeDtypeStruct(boxes, BF),
            jax.ShapeDtypeStruct(sides, BF),
            jax.ShapeDtypeStruct(boxes, BF),
        ),
        in_specs=[HBM] * 14,
        out_specs=(VMEM,) * 7,
        scratch_shapes=[
            pltpu.VMEM((3, WIDTH), BF),
            pltpu.VMEM((PROBES, WIDTH), F32),
            pltpu.VMEM((BOXES, NEAR), I32),
            pltpu.SMEM((BOXES,), I32),
            pltpu.VMEM((BOXES, POINTS, RANK), BF),
            pltpu.VMEM((BOXES, RANK, RANK), BF),
            pltpu.VMEM((1, RANK, RANK), BF),
            pltpu.VMEM((8, RANK, RANK), BF),
            pltpu.VMEM((1, FAR, RANK, RANK), BF),
            pltpu.VMEM((FAR, RANK, RANK), BF),
            pltpu.VMEM((1, FAR, RANK, RANK), BF),
            pltpu.SMEM((1, FAR), I32),
            pltpu.SMEM((8, FAR), I32),
            pltpu.SMEM((1, FAR), I32),
            pltpu.VMEM((32, POINTS), F32),
            pltpu.VMEM((32, POINTS), BF),
            pltpu.VMEM((64, POINTS), BF),
            pltpu.VMEM(boxes, F32),
            pltpu.VMEM((2, POINTS, POINTS), F32),
            pltpu.SMEM((8, 128), I32),
            pltpu.VMEM((FAR * RANK, RANK), BF),
            pltpu.VMEM((WIDTH, RANK), BF),
            pltpu.VMEM((LINE, PROBES, RANK), BF),
            pltpu.VMEM((LINES, 2, PROBES, RANK), BF),
            pltpu.VMEM((GX, PROBES, RANK), BF),
            pltpu.VMEM((LINE * LINES, PROBES, RANK), BF),
            dma((14,)),
            dma((1,)),
            dma((4,)),
            dma((4,)),
            dma((2,)),
            dma((2,)),
            dma((2,)),
            dma((2,)),
            dma((2,)),
        ],
        compiler_params=pltpu.CompilerParams(
            collective_id=0, has_side_effects=True, vmem_limit_bytes=VMEM_LIMIT
        ),
    )(*arrays)


def near_kernel(pairs_hbm, total, own_vec, side_vec, own_source, side_source, target, out, pairs, dist, sem):
    load = pltpu.make_async_copy(pairs_hbm, pairs, sem.at[0])
    load.start()
    out[...] = total[...]
    load.wait()
    own = jnp.maximum(pairs[6, 0] - OWN_DONE, 0)
    side = jnp.maximum(pairs[7, 0] - SIDE_DONE, 0)

    def measure(row, source, task):
        lane = jnp.minimum(task, 127)
        return squares(source[pairs[row + 1, lane]], target[pairs[row, lane]])

    def add(row, vec, task, square):
        lanes = pl.ds(pl.multiple_of(pairs[row, task] * POINTS, POINTS), POINTS)
        weight = pairs[row + 2, task].astype(F32) * SCALE
        out[:, lanes] += weight * dot(vec[pairs[row + 1, task]], tile_of(square))

    def single(n, carry):
        add(0, own_vec, OWN_DONE + n, measure(0, own_source, OWN_DONE + n))
        return carry

    lax.fori_loop(0, own, single, 0)

    dist[0] = measure(3, side_source, SIDE_DONE)

    def turns(width, first):
        def turn(n, carry):
            for k in range(width):
                task = first + n * width + k
                square = dist[k % 2]
                dist[1 - k % 2] = measure(3, side_source, task + 1)
                add(3, side_vec, task, square)
            return carry

        return turn

    whole = side // TURN
    rest = side % TURN
    lax.fori_loop(0, whole, turns(TURN, SIDE_DONE), 0)
    lax.fori_loop(0, rest // 2, turns(2, SIDE_DONE + whole * TURN), 0)
    lax.fori_loop(0, rest % 2, turns(1, SIDE_DONE + side - 1), 0)


def near_field(total, pairs, *arrays):
    return pl.pallas_call(
        near_kernel,
        out_shape=jax.ShapeDtypeStruct((PROBES, WIDTH), F32),
        in_specs=[ANY] + [VMEM] * 6,
        out_specs=VMEM,
        scratch_shapes=[
            pltpu.SMEM((8, 128), I32),
            pltpu.VMEM((2, POINTS, POINTS), F32),
            pltpu.SemaphoreType.DMA((1,)),
        ],
        compiler_params=pltpu.CompilerParams(vmem_limit_bytes=VMEM_LIMIT),
    )(pairs, total, *arrays)


def local(gy_count, coords, vectors, *rest):
    matrices, near_list, near_count = rest[:-2], rest[-2], rest[-1]
    arrays = (coords, vectors, near_list, near_count, *matrices)
    return near_field(*far_field(gy_count, *(pltpu.with_memory_space_constraint(a, pltpu.HBM) for a in arrays)))


def solution(mesh):
    both = ("gx", "gy")
    return jax.shard_map(
        functools.partial(local, mesh.shape["gy"]),
        mesh=mesh,
        in_specs=(
            P(None, both),
            P(None, both),
            P(both, None, None),
            P(both, None, None),
            P(both, None, None),
            P("gx", None, None),
            P(both, None, None, None),
            P("gx", None, None, None),
            P("gx", None, None, None),
            P(both, None),
            P("gx", None),
            P("gx", None),
            P(both, None),
            P(both),
        ),
        out_specs=P(None, both),
        check_vma=False,
    )
```
